32 devices in a mesh: band: 4 (over y, x), fft: 8 (over z, core).
Axes of the slice: x: 2, y: 2, z: 4, core: 2. Of those that a mesh axis runs over, the one named last changes fastest.
Arguments:
- coeff: bfloat16 [8, 256, 256, 256], P('band', None, 'fft'), may hold values from -6 to 6
- sphere: int32 [256, 256, 256], P(None, 'fft'), may hold values from 0 to 1, as said below
- potential: float32 [256, 256, 256], P('fft'), may hold values from -2 to 0.5
- proj_values: bfloat16 [4096, 4, 128], P('fft', None, 'band'), may hold values from -0.59765625 to 0.59765625
- tile_cell: int32 [4096], P('fft'), may hold values from 0 to 16383
- tile_atom: int32 [4096], P('fft'), may hold values from 0 to 127, as said below
- tile_count: int32 [8], P('fft'), may hold values from 64 to 512, as said below
- dion: float32 [4], replicated, may hold values from 0.3 to 3
Outputs:
- hpsi: bfloat16 [8, 256, 256, 256], P('band', None, 'fft')
The draws below stay inside these ranges and needn't reach their ends.
Inputs may be any that keep to these rules, and one draw needn't show every extreme that they name: sphere is 1 exactly where (kx * S / 256)^2 + (ky * S / 256)^2 + (kz * S / 256)^2 < R, with kx, ky, kz the frequencies freq of the three indices, S the largest of 256, 256, 256, and R drawn from S*S/32 to S*S/16 - 1; so every frequency with sphere 1 is under a quarter of its length. `tile_atom`: a slot of slab f names an atom a with a // 16 within 3 slabs of f, counted around the periodic cell. `tile_count`: one slab is full in every draw; the others hold 64 to 256 live slots.
All inputs are finite; a program needn't handle non-finite values.
Results may differ from the reference program's by a relative error of at most 0.008.
The reference program's roundings to bfloat16 on the way count: a program that leaves them out, or rounds other values in their place, can miss the bound.
Values may be sent and summed in bfloat16 or wider, within the bound.
A program may use at most 128 MiB of HBM per device.

```python
import math
import jax
import jax.numpy as jnp
from jax import lax

NX = 256
NY = 256
NZ = 256
ORBS = 8
NPROJ = 4
APD = 16
ATOMS = 128
REACH = 3
TILES_DEV = 512
TILES = 4096
TPOS = 16384
N_FFT = 8


def draw_sphere(key, part):
    key = jax.random.fold_in(key, 11)
    largest = max(NX, max(NY, NZ))
    radius = jax.random.randint(key, (), largest * largest // 32, largest * largest // 16, dtype=jnp.int32)
    index_x = jnp.arange(NX, dtype=jnp.int32)
    index_y = jnp.arange(NY, dtype=jnp.int32)
    index_z = jnp.arange(NZ, dtype=jnp.int32)
    scaled_x = jnp.minimum(index_x, NX - index_x) * (largest // NX)
    scaled_y = jnp.minimum(index_y, NY - index_y) * (largest // NY)
    scaled_z = jnp.minimum(index_z, NZ - index_z) * (largest // NZ)
    total = (scaled_x * scaled_x)[:, None, None] + (scaled_y * scaled_y)[None, :, None] + (scaled_z * scaled_z)[None, None, :]
    return (total < radius).astype(jnp.int32)


def draw_tile_atom(key, part):
    key = jax.random.fold_in(key, 23)
    key_off, key_in = jax.random.split(key)
    slab_of = jnp.arange(TILES, dtype=jnp.int32) // TILES_DEV
    offset = jax.random.randint(key_off, (TILES,), -REACH, REACH + 1, dtype=jnp.int32)
    inner = jax.random.randint(key_in, (TILES,), 0, APD, dtype=jnp.int32)
    return ((slab_of + offset) % N_FFT * APD + inner).astype(jnp.int32)


def draw_tile_count(key, part):
    key = jax.random.fold_in(key, 37)
    key_base, key_full = jax.random.split(key)
    base = jax.random.randint(key_base, (N_FFT,), TILES_DEV // 8, TILES_DEV // 2 + 1, dtype=jnp.int32)
    full = jax.random.randint(key_full, (), 0, N_FFT, dtype=jnp.int32)
    return jnp.where(jnp.arange(N_FFT, dtype=jnp.int32) == full, TILES_DEV, base).astype(jnp.int32)


def plant(result, rng, least, high):
    longest = result.shape.index(max(result.shape))
    spots = []
    for shift in (0, 1):
        where = [jax.random.randint(jax.random.fold_in(rng, axis), (), 0, length) for axis, length in enumerate(result.shape)]
        where[longest] = (where[longest] + shift) % result.shape[longest]
        spots.append(tuple(where))
    return result.at[spots[0]].set(least).at[spots[1]].set(high)


def steps_of(rng, dims, cuts, least, high):
    level, own = 1.0, jax.random.fold_in(rng, 6)
    for axis_at, parts in cuts:
        draws = jnp.exp(jax.random.uniform(jax.random.fold_in(own, axis_at), (parts,), jnp.float32, least / len(cuts), high / len(cuts)))
        level = level * jnp.repeat(draws, dims[axis_at] // parts).reshape([-1 if axis == axis_at else 1 for axis in range(len(dims))])
    return level


def normal_values(rng, dims, spread, most, pieces=(), held_as=jnp.bfloat16):
    entries = jax.random.normal(rng, dims, jnp.float32) * spread
    if len(pieces) > 0:
        entries = steps_of(rng, dims, pieces, -0.22, 0.18) * entries
    return jnp.clip(entries, min=-most, max=most).astype(held_as)


def setup_inputs(seed: int = 0) -> dict:
    splits = jax.random.split(jax.random.key(seed), 9)
    coeff = normal_values(splits[0], (ORBS, NX, NY, NZ), 1.0, 6.0, ((0, 4), (2, 8)))
    sphere = draw_sphere(jax.random.fold_in(splits[8], 71), 0)
    potential = jnp.clip(-2.0 + 2.5 * jax.random.uniform(splits[2], (NX, NY, NZ), jnp.float32) ** steps_of(splits[2], (NX, NY, NZ), ((0, 8),), -0.2, 0.2), -2.0, 0.5)
    proj_values = normal_values(splits[3], (TILES, NPROJ, 128), 0.1, 0.59765625, ((0, 8), (2, 4)))
    tile_cell = plant(jax.random.randint(splits[4], (TILES,), 0, TPOS), jax.random.fold_in(splits[4], 1), 0, TPOS - 1).astype(jnp.int32)
    tile_atom = draw_tile_atom(jax.random.fold_in(splits[8], 71), 0)
    tile_count = draw_tile_count(jax.random.fold_in(splits[8], 71), 0)
    dion = jnp.clip(jnp.exp(jax.random.uniform(splits[7], (NPROJ,), jnp.float32, math.log(0.3), math.log(3.0))), 0.3, 3.0)
    return dict(coeff=coeff, sphere=sphere, potential=potential, proj_values=proj_values, tile_cell=tile_cell, tile_atom=tile_atom, tile_count=tile_count, dion=dion)


def cas_table(length):
    index = jnp.arange(length, dtype=jnp.int32)
    product = index[:, None] * index[None, :] % length
    angle = product.astype(jnp.float32) * (2.0 * math.pi / length)
    return ((jnp.cos(angle) + jnp.sin(angle)) * (1.0 / math.sqrt(length))).astype(jnp.bfloat16)

def frequency(index, length):
    return jnp.minimum(index, length - index)

def reference(coeff, sphere, potential, proj_values, tile_cell, tile_atom, tile_count, dion):
    high = lax.Precision.HIGHEST
    table_x = cas_table(NX).astype(jnp.float32)
    table_y = cas_table(NY).astype(jnp.float32)
    table_z = cas_table(NZ).astype(jnp.float32)
    row_x = frequency(jnp.arange(NX, dtype=jnp.int32), NX).astype(jnp.float32)
    row_y = frequency(jnp.arange(NY, dtype=jnp.int32), NY).astype(jnp.float32)
    row_z = frequency(jnp.arange(NZ, dtype=jnp.int32), NZ).astype(jnp.float32)
    kinetic = 2.0 * ((4.0 * row_x / NX)[:, None, None] ** 2 + (4.0 * row_y / NY)[None, :, None] ** 2 + (4.0 * row_z / NZ)[None, None, :] ** 2)
    sphere_real = sphere.astype(jnp.float32)
    slot_index = jnp.arange(TILES, dtype=jnp.int32)
    slab_of = slot_index // TILES_DEV
    live = (slot_index % TILES_DEV < tile_count[slab_of]).astype(jnp.float32)
    position = slab_of * TPOS + tile_cell
    proj_real = proj_values.astype(jnp.float32)

    def one_orbital(orbital):
        masked = (orbital.astype(jnp.float32) * sphere_real).astype(jnp.bfloat16)
        section_one = jnp.einsum('ax,xyz->ayz', table_x, masked.astype(jnp.float32), precision=high).astype(jnp.bfloat16)
        section_two = jnp.einsum('by,xyz->xbz', table_y, section_one.astype(jnp.float32), precision=high).astype(jnp.bfloat16)
        real = jnp.einsum('xyk,kz->xyz', section_two.astype(jnp.float32), table_z, precision=high).astype(jnp.bfloat16)
        flat = real.reshape(N_FFT * TPOS, 128)
        patches = flat[position].astype(jnp.float32)
        partial_value = jnp.einsum('tc,tpc->tp', patches, proj_real, precision=high) * live[:, None]
        intersection = jax.ops.segment_sum(partial_value, tile_atom, num_segments=ATOMS)
        back = (intersection * dion[None, :])[tile_atom] * live[:, None]
        added = jnp.einsum('tp,tpc->tc', back, proj_real, precision=high)
        nonlocal_part = jnp.zeros((N_FFT * TPOS, 128), jnp.float32).at[position].add(added).reshape(NX, NY, NZ)
        mixed = (potential * real.astype(jnp.float32) + nonlocal_part).astype(jnp.bfloat16)
        section_three = jnp.einsum('xyz,zk->xyk', mixed.astype(jnp.float32), table_z, precision=high).astype(jnp.bfloat16)
        section_four = jnp.einsum('by,xyz->xbz', table_y, section_three.astype(jnp.float32), precision=high).astype(jnp.bfloat16)
        spectrum = jnp.einsum('ax,xyz->ayz', table_x, section_four.astype(jnp.float32), precision=high)
        return (sphere_real * (spectrum + kinetic * masked.astype(jnp.float32))).astype(jnp.bfloat16)
    return lax.map(one_orbital, coeff)
```

```python
import math

import jax
import jax.numpy as jnp
from jax import lax
from jax.experimental import pallas as pl
from jax.experimental.pallas import tpu as pltpu
from jax.sharding import PartitionSpec as P

APD = 16
REACH = 3
MESH = pl.DeviceIdType.MESH
VMEM_BYTES = 58 * 2**20


def from_behind(value, axis, steps):
    count = lax.axis_size(axis)
    pairs = [(source, (source + steps) % count) for source in range(count)]
    return lax.ppermute(value, axis, pairs)


def cas_table(length):
    index = jnp.arange(length, dtype=jnp.int32)
    product = index[:, None] * index[None, :] % length
    angle = product.astype(jnp.float32) * (2.0 * math.pi / length)
    return ((jnp.cos(angle) + jnp.sin(angle)) * (1.0 / math.sqrt(length))).astype(jnp.bfloat16)


def frequency(index, length):
    return jnp.minimum(index, length - index)


def general(coeff, sphere, potential, proj_values, tile_cell, tile_atom, tile_count, dion):
    high = lax.Precision.HIGHEST
    orbitals, full_x, local_y, full_z = coeff.shape
    shards = lax.axis_size("fft")
    own_index = lax.axis_index("fft")
    full_y = local_y * shards
    table_x = cas_table(full_x)
    table_y = cas_table(full_y)
    table_z = cas_table(full_z)
    sphere_real = sphere.astype(jnp.float32)
    masked = (coeff.astype(jnp.float32) * sphere_real[None]).astype(jnp.bfloat16)
    row_x = frequency(jnp.arange(full_x, dtype=jnp.int32), full_x).astype(jnp.float32)
    row_y = frequency(own_index * local_y + jnp.arange(local_y, dtype=jnp.int32), full_y).astype(
        jnp.float32
    )
    row_z = frequency(jnp.arange(full_z, dtype=jnp.int32), full_z).astype(jnp.float32)
    kinetic = 2.0 * (
        (4.0 * row_x / full_x)[:, None, None] ** 2
        + (4.0 * row_y / full_y)[None, :, None] ** 2
        + (4.0 * row_z / full_z)[None, None, :] ** 2
    )
    section_one = jnp.einsum(
        "ax,oxyz->oayz", table_x, masked, preferred_element_type=jnp.float32
    ).astype(jnp.bfloat16)
    along_y = jnp.einsum(
        "by,oxyz->oxbz",
        table_y,
        lax.all_to_all(section_one, "fft", split_axis=1, concat_axis=2, tiled=True),
        preferred_element_type=jnp.float32,
    ).astype(jnp.bfloat16)
    real = jnp.dot(along_y, table_z, preferred_element_type=jnp.float32).astype(jnp.bfloat16)
    whole_proj = lax.all_gather(proj_values, "band", axis=2, tiled=True)
    flat = real.reshape(orbitals, -1, 128)
    patches = jnp.take(flat, tile_cell, axis=1)
    slots = tile_cell.shape[0]
    live = (jnp.arange(slots, dtype=jnp.int32) < tile_count[0]).astype(jnp.float32)
    partial_value = (
        jnp.einsum("otc,tpc->otp", patches, whole_proj, preferred_element_type=jnp.float32)
        * live[None, :, None]
    )
    width = (2 * REACH + 1) * APD
    home = tile_atom // APD
    local_atom = (home - own_index + REACH) % shards * APD + tile_atom % APD
    onehot = (local_atom[:, None] == jnp.arange(width, dtype=jnp.int32)[None, :]).astype(
        jnp.float32
    )
    table = jnp.einsum("otp,ta->oap", partial_value, onehot, precision=high)
    intersection = table
    for offset in range(-2 * REACH, 2 * REACH + 1):
        if offset != 0:
            arrived = from_behind(table, "fft", offset)
            first = max(0, -offset)
            last = min(2 * REACH, 2 * REACH - offset)
            intersection = intersection.at[:, first * APD : (last + 1) * APD].add(
                arrived[:, (first + offset) * APD : (last + offset + 1) * APD]
            )
    weights = intersection * dion[None, None, :]
    back = jnp.einsum("oap,ta->otp", weights, onehot, precision=high) * live[None, :, None]
    added = jnp.einsum("otp,tpc->otc", back, whole_proj.astype(jnp.float32), precision=high)
    nonlocal_part = (
        jnp.zeros(flat.shape, jnp.float32).at[:, tile_cell].add(added).reshape(real.shape)
    )
    mixed = (potential[None] * real.astype(jnp.float32) + nonlocal_part).astype(jnp.bfloat16)
    section_three = jnp.dot(mixed, table_z, preferred_element_type=jnp.float32).astype(jnp.bfloat16)
    section_four = jnp.einsum(
        "by,oxyz->oxbz", table_y, section_three, preferred_element_type=jnp.float32
    ).astype(jnp.bfloat16)
    spectrum = jnp.einsum(
        "ax,oxyz->oayz",
        table_x,
        lax.all_to_all(section_four, "fft", split_axis=2, concat_axis=1, tiled=True),
        preferred_element_type=jnp.float32,
    )
    result = sphere_real[None] * (spectrum + kinetic[None] * masked.astype(jnp.float32))
    return result.astype(jnp.bfloat16)


def remote(source, target, send_sem, recv_sem, device):
    return pltpu.make_async_remote_copy(
        src_ref=source,
        dst_ref=target,
        send_sem=send_sem,
        recv_sem=recv_sem,
        device_id={"fft": device},
        device_id_type=MESH,
    )


def greet(device):
    pl.semaphore_signal(
        pltpu.get_barrier_semaphore(), inc=1, device_id={"fft": device}, device_id_type=MESH
    )


CHUNKS = 8


def spread_kernel(own, out, local_sem, send_on, send_side, recv_on, recv_side):
    me = lax.axis_index("fft")
    chip, core = me // 2, me % 2
    sibling = me + 1 - 2 * core
    below = jnp.maximum(me - 2, core)
    above = jnp.minimum(me + 2, 6 + core)
    greet(sibling)

    @pl.when(chip > 0)
    def _():
        greet(below)

    @pl.when(chip < 3)
    def _():
        greet(above)

    pl.semaphore_wait(pltpu.get_barrier_semaphore(), 1 + jnp.minimum(chip, 1) + jnp.minimum(3 - chip, 1))

    def piece(ref, k):
        return ref.at[k // 4, pl.ds(k % 4 * 8, 8)]

    def slot(block, k):
        return out.at[k // 4, block, pl.ds(k % 4 * 8, 8)]

    for way, edge in ((0, 0), (1, 3)):

        @pl.when(chip == edge)
        def _(way=way):
            for orbital in range(2):
                pltpu.make_async_copy(
                    own.at[orbital], out.at[orbital, 2 * way + core], local_sem.at[orbital]
                ).start()

    def step(k, carry):
        for way, edge, onward in ((0, 0, above), (1, 3, below)):
            here = slot(2 * way + core, k)

            def pass_on(source, last, way=way, here=here, onward=onward):
                if not last:
                    remote(source, here, send_on.at[way, k], recv_on.at[way, k], onward).start()
                remote(source, here, send_side.at[way, k], recv_side.at[way, k], sibling).start()

            def arrived(way=way, here=here, onward=onward):
                remote(here, here, send_on.at[way, k], recv_on.at[way, k], onward).wait_recv()

            @pl.when(chip == edge)
            def _(pass_on=pass_on):
                pass_on(piece(own, k), False)

            @pl.when((chip > 0) & (chip < 3))
            def _(pass_on=pass_on, arrived=arrived, here=here):
                arrived()
                pass_on(here, False)

            @pl.when(chip == 3 - edge)
            def _(pass_on=pass_on, arrived=arrived, here=here):
                arrived()
                pass_on(here, True)

        return carry

    lax.fori_loop(0, CHUNKS, step, 0)

    def finish(k, carry):
        for way, edge, onward in ((0, 0, above), (1, 3, below)):
            here = slot(2 * way + core, k)
            there = slot(2 * way + 1 - core, k)
            side = remote(there, there, send_side.at[way, k], recv_side.at[way, k], sibling)
            side.wait_recv()
            remote(here, here, send_side.at[way, k], recv_side.at[way, k], sibling).wait_send()

            @pl.when(chip != 3 - edge)
            def _(way=way, here=here, onward=onward):
                remote(here, here, send_on.at[way, k], recv_on.at[way, k], onward).wait_send()

        return carry

    lax.fori_loop(0, CHUNKS, finish, 0)
    for way, edge in ((0, 0), (1, 3)):

        @pl.when(chip == edge)
        def _(way=way):
            for orbital in range(2):
                pltpu.make_async_copy(
                    own.at[orbital], out.at[orbital, 2 * way + core], local_sem.at[orbital]
                ).wait()


def spread(own):
    return pl.pallas_call(
        spread_kernel,
        out_shape=jax.ShapeDtypeStruct((2, 4, 32, 128, 128), jnp.bfloat16),
        in_specs=[pl.BlockSpec(memory_space=pl.ANY)],
        out_specs=pl.BlockSpec(memory_space=pl.ANY),
        scratch_shapes=[pltpu.SemaphoreType.DMA((2,))] + [pltpu.SemaphoreType.DMA((2, CHUNKS))] * 4,
        compiler_params=pltpu.CompilerParams(collective_id=0, has_side_effects=True),
        name="spread",
    )(own)


def total_kernel(own, scale, out, slots, send_sem, recv_sem):
    me = lax.axis_index("fft")
    for step in range(1, 8):
        greet((me + step) % 8)
    pl.semaphore_wait(pltpu.get_barrier_semaphore(), 7)
    for step in range(1, 8):
        remote(own, slots.at[me], send_sem.at[step], recv_sem.at[step], (me + step) % 8).start()
    slots[me] = own[...]
    for step in range(1, 8):
        source = slots.at[(me + 8 - step) % 8]
        copy = remote(own, source, send_sem.at[step], recv_sem.at[step], (me + step) % 8)
        copy.wait_recv()
        copy.wait_send()
    total = slots[0]
    for step in range(1, 8):
        total = total + slots[step]
    out[...] = total * scale[...]


def total(own, scale):
    return pl.pallas_call(
        total_kernel,
        out_shape=jax.ShapeDtypeStruct(own.shape, jnp.float32),
        in_specs=[pl.BlockSpec(memory_space=pltpu.VMEM)] * 2,
        out_specs=pl.BlockSpec(memory_space=pltpu.VMEM),
        scratch_shapes=[
            pltpu.VMEM((8,) + own.shape, jnp.float32),
            pltpu.SemaphoreType.DMA((8,)),
            pltpu.SemaphoreType.DMA((8,)),
        ],
        compiler_params=pltpu.CompilerParams(collective_id=1, has_side_effects=True),
        name="total",
    )(own, scale)


OWNERS = (0, 1, 6, 7)


def collect_kernel(own, out, local_sem, send_sem, recv_sem):
    me = lax.axis_index("fft")
    is_owner = (me < 2) | (me >= 6)

    @pl.when(is_owner)
    def _():
        for step in range(1, 8):
            greet((me + step) % 8)

    pl.semaphore_wait(pltpu.get_barrier_semaphore(), 4 - is_owner.astype(jnp.int32))
    rows = pl.ds(pl.multiple_of(me * 32, 32), 32)

    for block, owner in enumerate(OWNERS):
        for orbital in range(2):
            source = own.at[orbital, block]
            target = out.at[orbital, :, rows]

            @pl.when(me != owner)
            def _(source=source, target=target, block=block, orbital=orbital, owner=owner):
                remote(
                    source, target, send_sem.at[orbital, block], recv_sem.at[orbital, me], owner
                ).start()

            @pl.when(me == owner)
            def _(source=source, target=target, orbital=orbital):
                pltpu.make_async_copy(source, target, local_sem.at[orbital]).start()

    for block, owner in enumerate(OWNERS):
        for orbital in range(2):
            source = own.at[orbital, block]
            target = out.at[orbital, :, rows]

            @pl.when(me != owner)
            def _(source=source, target=target, block=block, orbital=orbital, owner=owner):
                remote(
                    source, target, send_sem.at[orbital, block], recv_sem.at[orbital, me], owner
                ).wait_send()

            @pl.when(me == owner)
            def _(source=source, target=target, orbital=orbital):
                pltpu.make_async_copy(source, target, local_sem.at[orbital]).wait()

    @pl.when(is_owner)
    def _():
        for step in range(1, 8):
            sender = (me + step) % 8
            for orbital in range(2):
                theirs = out.at[orbital, :, pl.ds(pl.multiple_of(sender * 32, 32), 32)]
                remote(
                    own.at[orbital, 0],
                    theirs,
                    send_sem.at[orbital, 0],
                    recv_sem.at[orbital, sender],
                    sender,
                ).wait_recv()


def collect(own):
    return pl.pallas_call(
        collect_kernel,
        out_shape=jax.ShapeDtypeStruct((2, 32, 256, 128), jnp.bfloat16),
        in_specs=[pl.BlockSpec(memory_space=pl.ANY)],
        out_specs=pl.BlockSpec(memory_space=pl.ANY),
        scratch_shapes=[
            pltpu.SemaphoreType.DMA((2,)),
            pltpu.SemaphoreType.DMA((2, 4)),
            pltpu.SemaphoreType.DMA((2, 8)),
        ],
        compiler_params=pltpu.CompilerParams(collective_id=2, has_side_effects=True),
        name="collect",
    )(own)


def matmul(left, right):
    return jnp.dot(left, right, preferred_element_type=jnp.float32)


def swap(value):
    return jnp.transpose(value, (1, 0, 2))


def grid_kernel(
    place, count, rows, table_x, table_y, table_z, proj, atom, real, sums, first, cells, patches
):
    table = table_x[...]

    def along_x(group, carry):
        block, inner = group // 4, group % 4
        found = [matmul(table, rows[0, block, inner * 8 + k]) for k in range(8)]
        first[:, pl.ds(pl.multiple_of(group * 8, 8), 8), :] = swap(jnp.stack(found))
        return carry

    lax.fori_loop(0, 16, along_x, 0)

    def plane(x, carry):
        second = matmul(table_y[...], first[x].astype(jnp.bfloat16)).astype(jnp.bfloat16)
        value = matmul(second, table_z[...]).astype(jnp.bfloat16)
        real[0, x] = value
        wide = value.astype(jnp.float32)
        base = pl.multiple_of(x * 512, 512)
        cells[pl.ds(base, 256), :] = wide[:, :128]
        cells[pl.ds(base + 256, 256), :] = wide[:, 128:]
        return carry

    lax.fori_loop(0, 32, plane, 0)

    def fetch(group, carry):
        base = pl.multiple_of(group * 8, 8)
        for k in range(8):
            patches[pl.ds(base + k, 1), :] = cells[pl.ds(place[base + k], 1), :]
        return carry

    lax.fori_loop(0, 64, fetch, 0)
    high = lax.Precision.HIGHEST
    atoms = lax.broadcasted_iota(jnp.int32, (128, 512), 0)
    slots = lax.broadcasted_iota(jnp.int32, (128, 512), 1)
    chosen = ((atoms == atom[...]) & (slots < count[0])).astype(jnp.float32)
    ones = jnp.ones((8, 128), jnp.float32)
    for p in range(4):
        product = patches[...] * proj[p].astype(jnp.float32)
        by_atom = jnp.dot(chosen, product, precision=high, preferred_element_type=jnp.float32)
        summed = lax.dot_general(
            ones, by_atom, (((1,), (1,)), ((), ())), precision=high, preferred_element_type=jnp.float32
        )
        sums[0, p : p + 1, :] = summed[0:1]


def whole(shape):
    return pl.BlockSpec(shape, lambda *_: (0,) * len(shape), pipeline_mode=pl.Buffered(1))


def to_grid(place, count, rows, table_x, table_y, table_z, proj, atom):
    smem = pl.BlockSpec(memory_space=pltpu.SMEM)
    return pl.pallas_call(
        grid_kernel,
        grid=(2,),
        out_shape=(
            jax.ShapeDtypeStruct((2, 32, 256, 256), jnp.bfloat16),
            jax.ShapeDtypeStruct((2, 4, 128), jnp.float32),
        ),
        in_specs=[
            smem,
            smem,
            pl.BlockSpec((1, 4, 32, 128, 128), lambda o: (o, 0, 0, 0, 0)),
            whole((32, 128)),
            whole((256, 128)),
            whole((128, 256)),
            whole((4, 512, 128)),
            whole((1, 512)),
        ],
        out_specs=(
            pl.BlockSpec((1, 32, 256, 256), lambda o: (o, 0, 0, 0)),
            pl.BlockSpec((1, 4, 128), lambda o: (o, 0, 0)),
        ),
        scratch_shapes=[
            pltpu.VMEM((32, 128, 128), jnp.float32),
            pltpu.VMEM((16384, 128), jnp.float32),
            pltpu.VMEM((512, 128), jnp.float32),
        ],
        compiler_params=pltpu.CompilerParams(vmem_limit_bytes=VMEM_BYTES),
        name="to_grid",
    )(place, count, rows, table_x, table_y, table_z, proj, atom)


def product_kernel(
    place, count, real, potential, weights, proj, atom, table_z, table_y, out, cells, added, fourth
):
    def multiply(x, carry):
        value = potential[x] * real[0, x].astype(jnp.float32)
        base = pl.multiple_of(x * 512, 512)
        cells[pl.ds(base, 256), :] = value[:, :128]
        cells[pl.ds(base + 256, 256), :] = value[:, 128:]
        return carry

    lax.fori_loop(0, 32, multiply, 0)
    atoms = lax.broadcasted_iota(jnp.int32, (512, 128), 1)
    slots = lax.broadcasted_iota(jnp.int32, (512, 128), 0)
    chosen = ((atoms == atom[...]) & (slots < count[0])).astype(jnp.float32)
    strength = jnp.concatenate([weights[0], weights[0]], axis=0)
    back = lax.dot_general(
        chosen,
        strength,
        (((1,), (1,)), ((), ())),
        precision=lax.Precision.HIGHEST,
        preferred_element_type=jnp.float32,
    )
    patch = back[:, 0:1] * proj[0].astype(jnp.float32)
    for p in range(1, 4):
        patch = patch + back[:, p : p + 1] * proj[p].astype(jnp.float32)
    added[...] = patch

    def store(group, carry):
        base = pl.multiple_of(group * 8, 8)
        for k in range(8):
            row = pl.ds(place[base + k], 1)
            cells[row, :] = cells[row, :] + added[pl.ds(base + k, 1), :]
        return carry

    lax.fori_loop(0, 64, store, 0)

    def plane(x, carry):
        base = pl.multiple_of(x * 512, 512)
        low = cells[pl.ds(base, 256), :].astype(jnp.bfloat16)
        top = cells[pl.ds(base + 256, 256), :].astype(jnp.bfloat16)
        third = matmul(jnp.concatenate([low, top], axis=1), table_z[...]).astype(jnp.bfloat16)
        fourth[x] = matmul(table_y[...], third)
        return carry

    lax.fori_loop(0, 32, plane, 0)

    def turn(group, carry):
        block, inner = group // 4, group % 4
        value = fourth[:, pl.ds(pl.multiple_of(group * 8, 8), 8), :]
        out[0, block, pl.ds(inner * 8, 8)] = swap(value).astype(jnp.bfloat16)
        return carry

    lax.fori_loop(0, 16, turn, 0)


def from_grid(place, count, real, potential, weights, proj, atom, table_z, table_y):
    smem = pl.BlockSpec(memory_space=pltpu.SMEM)
    return pl.pallas_call(
        product_kernel,
        grid=(2,),
        out_shape=jax.ShapeDtypeStruct((2, 4, 32, 32, 128), jnp.bfloat16),
        in_specs=[
            smem,
            smem,
            pl.BlockSpec((1, 32, 256, 256), lambda o: (o, 0, 0, 0)),
            whole((32, 256, 256)),
            pl.BlockSpec((1, 4, 128), lambda o: (o, 0, 0)),
            whole((4, 512, 128)),
            whole((512, 1)),
            whole((256, 128)),
            whole((128, 256)),
        ],
        out_specs=pl.BlockSpec((1, 4, 32, 32, 128), lambda o: (o, 0, 0, 0, 0)),
        scratch_shapes=[
            pltpu.VMEM((16384, 128), jnp.float32),
            pltpu.VMEM((512, 128), jnp.float32),
            pltpu.VMEM((32, 128, 128), jnp.float32),
        ],
        compiler_params=pltpu.CompilerParams(vmem_limit_bytes=VMEM_BYTES),
        name="from_grid",
    )(place, count, real, potential, weights, proj, atom, table_z, table_y)


def last_kernel(index, rows, table_x, coeff, sphere, out):
    block, orbital = pl.program_id(0), pl.program_id(1)
    shard = index[0]
    used = ((block < 2) | (block >= 6)) & ((shard < 2) | (shard >= 6))

    @pl.when(jnp.logical_not(used))
    def _():
        out[...] = jnp.zeros_like(out)

    def squares(start, shape, axis):
        at = lax.broadcasted_iota(jnp.int32, shape, axis) + start
        return (frequency(at, 256).astype(jnp.float32) * (4.0 / 256)) ** 2

    @pl.when(used)
    def _():
        table = table_x[...]
        for group in range(2):
            here = slice(group * 16, group * 16 + 16)
            found = [matmul(table, rows[orbital, group * 16 + k]) for k in range(16)]
            spectrum = swap(jnp.stack(found))
            kin_xy = squares(block * 32, (32, 16, 128), 0) + squares(
                shard * 32 + group * 16, (32, 16, 128), 1
            )
            for half in range(2):
                lanes = slice(half * 128, half * 128 + 128)
                ball = sphere[:, here, lanes].astype(jnp.float32)
                masked = coeff[0, :, here, lanes].astype(jnp.float32) * ball
                kinetic = 2.0 * (kin_xy + squares(half * 128, (32, 16, 128), 2))
                result = ball * (spectrum + kinetic * masked)
                out[0, :, here, lanes] = result.astype(jnp.bfloat16)


def last(index, rows, table_x, coeff, sphere):
    def used_block(b):
        return jnp.where((b >= 2) & (b < 6), 1, b)

    return pl.pallas_call(
        last_kernel,
        grid=(8, 2),
        out_shape=jax.ShapeDtypeStruct(coeff.shape, jnp.bfloat16),
        in_specs=[
            pl.BlockSpec(memory_space=pltpu.SMEM),
            whole((2, 32, 256, 128)),
            pl.BlockSpec((32, 256), lambda b, o: (used_block(b), 0)),
            pl.BlockSpec((1, 32, 32, 256), lambda b, o: (o, used_block(b), 0, 0)),
            pl.BlockSpec((32, 32, 256), lambda b, o: (used_block(b), 0, 0)),
        ],
        out_specs=pl.BlockSpec((1, 32, 32, 256), lambda b, o: (o, b, 0, 0)),
        compiler_params=pltpu.CompilerParams(vmem_limit_bytes=VMEM_BYTES),
        name="last",
    )(index, rows, table_x, coeff, sphere)


def used_rows(table):
    return jnp.concatenate([table[:64], table[192:]], axis=0)


def inner_mask(coeff, sphere):
    masked = (coeff.astype(jnp.float32) * sphere.astype(jnp.float32)[None]).astype(jnp.bfloat16)
    masked = jnp.concatenate([masked[:, :64], masked[:, 192:]], axis=1)
    near = jnp.arange(128, dtype=jnp.int32) < 64
    return jnp.where(near, masked[..., :128], masked[..., 128:])


def line_of_chips(coeff, sphere, potential, proj_values, tile_cell, tile_atom, tile_count, dion):
    own_index = lax.axis_index("fft")
    table = cas_table(256)
    part = used_rows(table)
    own_x = lax.dynamic_slice_in_dim(table, own_index * 32, 32, 0)
    own_x = used_rows(own_x.T).T
    proj = lax.all_gather(proj_values, "band", axis=2, tiled=True).transpose(1, 0, 2)
    place = tile_cell // 512 * 512 + tile_cell % 2 * 256 + tile_cell % 512 // 2
    rows = spread(inner_mask(coeff, sphere).transpose(0, 2, 1, 3))
    real, sums = to_grid(
        place, tile_count, rows, own_x, part.T, part, proj, tile_atom[None, :]
    )
    weights = total(sums, jnp.broadcast_to(dion[None, :, None], sums.shape))
    fourth = from_grid(
        place, tile_count, real, potential, weights, proj, tile_atom[:, None], part.T, part
    )
    return last(own_index[None], collect(fourth), table, coeff, sphere)


def local(*values):
    coeff, slots, shards = values[0], values[4].shape[0], lax.axis_size("fft")
    if coeff.shape == (2, 256, 32, 256) and shards == 8 and slots == 512:
        return line_of_chips(*values)
    return general(*values)


def solution(mesh):
    in_specs = (
        P("band", None, "fft", None),
        P(None, "fft", None),
        P("fft", None, None),
        P("fft", None, "band"),
        P("fft"),
        P("fft"),
        P("fft"),
        P(),
    )
    out_specs = P("band", None, "fft", None)
    return jax.shard_map(local, mesh=mesh, in_specs=in_specs, out_specs=out_specs, check_vma=False)
```

```python
import math

import jax
import jax.numpy as jnp
from jax import lax
from jax.experimental import pallas as pl
from jax.experimental.pallas import tpu as pltpu
from jax.sharding import PartitionSpec as P

APD = 16
REACH = 3
MESH = pl.DeviceIdType.MESH
VMEM_BYTES = 58 * 2**20


def from_behind(value, axis, steps):
    count = lax.axis_size(axis)
    pairs = [(source, (source + steps) % count) for source in range(count)]
    return lax.ppermute(value, axis, pairs)


def cas_table(length):
    index = jnp.arange(length, dtype=jnp.int32)
    product = index[:, None] * index[None, :] % length
    angle = product.astype(jnp.float32) * (2.0 * math.pi / length)
    return ((jnp.cos(angle) + jnp.sin(angle)) * (1.0 / math.sqrt(length))).astype(jnp.bfloat16)


def frequency(index, length):
    return jnp.minimum(index, length - index)


def general(coeff, sphere, potential, proj_values, tile_cell, tile_atom, tile_count, dion):
    high = lax.Precision.HIGHEST
    orbitals, full_x, local_y, full_z = coeff.shape
    shards = lax.axis_size("fft")
    own_index = lax.axis_index("fft")
    full_y = local_y * shards
    table_x = cas_table(full_x)
    table_y = cas_table(full_y)
    table_z = cas_table(full_z)
    sphere_real = sphere.astype(jnp.float32)
    masked = (coeff.astype(jnp.float32) * sphere_real[None]).astype(jnp.bfloat16)
    row_x = frequency(jnp.arange(full_x, dtype=jnp.int32), full_x).astype(jnp.float32)
    row_y = frequency(own_index * local_y + jnp.arange(local_y, dtype=jnp.int32), full_y).astype(
        jnp.float32
    )
    row_z = frequency(jnp.arange(full_z, dtype=jnp.int32), full_z).astype(jnp.float32)
    kinetic = 2.0 * (
        (4.0 * row_x / full_x)[:, None, None] ** 2
        + (4.0 * row_y / full_y)[None, :, None] ** 2
        + (4.0 * row_z / full_z)[None, None, :] ** 2
    )
    section_one = jnp.einsum(
        "ax,oxyz->oayz", table_x, masked, preferred_element_type=jnp.float32
    ).astype(jnp.bfloat16)
    along_y = jnp.einsum(
        "by,oxyz->oxbz",
        table_y,
        lax.all_to_all(section_one, "fft", split_axis=1, concat_axis=2, tiled=True),
        preferred_element_type=jnp.float32,
    ).astype(jnp.bfloat16)
    real = jnp.dot(along_y, table_z, preferred_element_type=jnp.float32).astype(jnp.bfloat16)
    whole_proj = lax.all_gather(proj_values, "band", axis=2, tiled=True)
    flat = real.reshape(orbitals, -1, 128)
    patches = jnp.take(flat, tile_cell, axis=1)
    slots = tile_cell.shape[0]
    live = (jnp.arange(slots, dtype=jnp.int32) < tile_count[0]).astype(jnp.float32)
    partial_value = (
        jnp.einsum("otc,tpc->otp", patches, whole_proj, preferred_element_type=jnp.float32)
        * live[None, :, None]
    )
    width = (2 * REACH + 1) * APD
    home = tile_atom // APD
    local_atom = (home - own_index + REACH) % shards * APD + tile_atom % APD
    onehot = (local_atom[:, None] == jnp.arange(width, dtype=jnp.int32)[None, :]).astype(
        jnp.float32
    )
    table = jnp.einsum("otp,ta->oap", partial_value, onehot, precision=high)
    intersection = table
    for offset in range(-2 * REACH, 2 * REACH + 1):
        if offset != 0:
            arrived = from_behind(table, "fft", offset)
            first = max(0, -offset)
            last = min(2 * REACH, 2 * REACH - offset)
            intersection = intersection.at[:, first * APD : (last + 1) * APD].add(
                arrived[:, (first + offset) * APD : (last + offset + 1) * APD]
            )
    weights = intersection * dion[None, None, :]
    back = jnp.einsum("oap,ta->otp", weights, onehot, precision=high) * live[None, :, None]
    added = jnp.einsum("otp,tpc->otc", back, whole_proj.astype(jnp.float32), precision=high)
    nonlocal_part = (
        jnp.zeros(flat.shape, jnp.float32).at[:, tile_cell].add(added).reshape(real.shape)
    )
    mixed = (potential[None] * real.astype(jnp.float32) + nonlocal_part).astype(jnp.bfloat16)
    section_three = jnp.dot(mixed, table_z, preferred_element_type=jnp.float32).astype(jnp.bfloat16)
    section_four = jnp.einsum(
        "by,oxyz->oxbz", table_y, section_three, preferred_element_type=jnp.float32
    ).astype(jnp.bfloat16)
    spectrum = jnp.einsum(
        "ax,oxyz->oayz",
        table_x,
        lax.all_to_all(section_four, "fft", split_axis=2, concat_axis=1, tiled=True),
        preferred_element_type=jnp.float32,
    )
    result = sphere_real[None] * (spectrum + kinetic[None] * masked.astype(jnp.float32))
    return result.astype(jnp.bfloat16)


def remote(source, target, send_sem, recv_sem, device):
    return pltpu.make_async_remote_copy(
        src_ref=source,
        dst_ref=target,
        send_sem=send_sem,
        recv_sem=recv_sem,
        device_id={"fft": device},
        device_id_type=MESH,
    )


def greet(device):
    pl.semaphore_signal(
        pltpu.get_barrier_semaphore(), inc=1, device_id={"fft": device}, device_id_type=MESH
    )


OWNERS = (0, 1, 6, 7)


def sections_kernel(owner, coeff_low, coeff_top, sphere_low, sphere_top, table_x, out, masked):
    @pl.when(owner[0] == 1)
    def _():
        near = lax.broadcasted_iota(jnp.int32, (64, 32, 128), 2) < 64
        for half, (coeff, sphere) in enumerate(((coeff_low, sphere_low), (coeff_top, sphere_top))):
            ball = sphere[...].astype(jnp.float32)
            value = coeff[0].astype(jnp.float32) * ball
            value = jnp.where(near, value[..., :128], value[..., 128:])
            masked[:, half * 64 : half * 64 + 64, :] = swap(value).astype(jnp.bfloat16)

        def along_x(block, carry):
            planes = pl.ds(pl.multiple_of(block * 64, 64), 64)
            table = table_x[planes, :]
            for group in range(2):
                found = [matmul(table, masked[group * 16 + k]) for k in range(16)]
                value = swap(jnp.stack(found)).astype(jnp.bfloat16)
                out[0, planes, group * 16 : group * 16 + 16, :] = value
            return carry

        lax.fori_loop(0, 4, along_x, 0)


def sections(owner, coeff, sphere, table_x):
    return pl.pallas_call(
        sections_kernel,
        grid_spec=pltpu.PrefetchScalarGridSpec(
            num_scalar_prefetch=1,
            grid=(2,),
            in_specs=[
                pl.BlockSpec((1, 64, 32, 256), lambda o, own: (o * own[0], 0, 0, 0)),
                pl.BlockSpec((1, 64, 32, 256), lambda o, own: (o * own[0], 3, 0, 0)),
                pl.BlockSpec((64, 32, 256), lambda o, own: (0, 0, 0)),
                pl.BlockSpec((64, 32, 256), lambda o, own: (3, 0, 0)),
                pl.BlockSpec((256, 128), lambda o, own: (0, 0)),
            ],
            out_specs=pl.BlockSpec((1, 256, 32, 128), lambda o, own: (o, 0, 0, 0)),
            scratch_shapes=[pltpu.VMEM((32, 128, 128), jnp.bfloat16)],
        ),
        out_shape=jax.ShapeDtypeStruct((2, 256, 32, 128), jnp.bfloat16),
        compiler_params=pltpu.CompilerParams(vmem_limit_bytes=VMEM_BYTES),
        name="sections",
    )(owner, coeff, coeff, sphere, sphere, table_x)


def spread_kernel(own, out, local_sem, send_sem, recv_sem):
    me = lax.axis_index("fft")
    is_owner = (me < 2) | (me >= 6)
    block = jnp.where(me < 2, me, me - 4)

    for owner in OWNERS:

        @pl.when(me != owner)
        def _(owner=owner):
            greet(owner)

    @pl.when(is_owner)
    def _():
        pl.semaphore_wait(pltpu.get_barrier_semaphore(), 7)

    def planes(device):
        return pl.ds(pl.multiple_of(device * 32, 32), 32)

    def slot(orbital, at):
        return out.at[orbital, :, pl.ds(pl.multiple_of(at * 32, 32), 32)]

    def outgoing(orbital, step):
        there = (me + step) % 8
        return remote(
            own.at[orbital, planes(there)],
            slot(orbital, block),
            send_sem.at[orbital, step],
            recv_sem.at[orbital, block],
            there,
        )

    def kept(orbital):
        return pltpu.make_async_copy(
            own.at[orbital, planes(me)], slot(orbital, block), local_sem.at[orbital]
        )

    @pl.when(is_owner)
    def _():
        for orbital in range(2):
            for step in range(1, 8):
                outgoing(orbital, step).start()
            kept(orbital).start()

    for at, owner in enumerate(OWNERS):

        @pl.when(me != owner)
        def _(at=at, owner=owner):
            for orbital in range(2):
                remote(
                    own.at[orbital, planes(0)],
                    slot(orbital, at),
                    send_sem.at[orbital, 0],
                    recv_sem.at[orbital, at],
                    owner,
                ).wait_recv()

    @pl.when(is_owner)
    def _():
        for orbital in range(2):
            for step in range(1, 8):
                outgoing(orbital, step).wait_send()
            kept(orbital).wait()


def spread(own):
    return pl.pallas_call(
        spread_kernel,
        out_shape=jax.ShapeDtypeStruct((2, 32, 128, 128), jnp.bfloat16),
        in_specs=[pl.BlockSpec(memory_space=pl.ANY)],
        out_specs=pl.BlockSpec(memory_space=pl.ANY),
        scratch_shapes=[
            pltpu.SemaphoreType.DMA((2,)),
            pltpu.SemaphoreType.DMA((2, 8)),
            pltpu.SemaphoreType.DMA((2, 4)),
        ],
        compiler_params=pltpu.CompilerParams(collective_id=0, has_side_effects=True),
        name="spread",
    )(own)


def total_kernel(own, scale, out, slots, send_sem, recv_sem):
    me = lax.axis_index("fft")
    for step in range(1, 8):
        greet((me + step) % 8)
    pl.semaphore_wait(pltpu.get_barrier_semaphore(), 7)
    for step in range(1, 8):
        remote(own, slots.at[me], send_sem.at[step], recv_sem.at[step], (me + step) % 8).start()
    slots[me] = own[...]
    for step in range(1, 8):
        source = slots.at[(me + 8 - step) % 8]
        copy = remote(own, source, send_sem.at[step], recv_sem.at[step], (me + step) % 8)
        copy.wait_recv()
        copy.wait_send()
    total = slots[0]
    for step in range(1, 8):
        total = total + slots[step]
    out[...] = total * scale[...]


def total(own, scale):
    return pl.pallas_call(
        total_kernel,
        out_shape=jax.ShapeDtypeStruct(own.shape, jnp.float32),
        in_specs=[pl.BlockSpec(memory_space=pltpu.VMEM)] * 2,
        out_specs=pl.BlockSpec(memory_space=pltpu.VMEM),
        scratch_shapes=[
            pltpu.VMEM((8,) + own.shape, jnp.float32),
            pltpu.SemaphoreType.DMA((8,)),
            pltpu.SemaphoreType.DMA((8,)),
        ],
        compiler_params=pltpu.CompilerParams(collective_id=1, has_side_effects=True),
        name="total",
    )(own, scale)


def collect_kernel(own, out, local_sem, send_sem, recv_sem):
    me = lax.axis_index("fft")
    is_owner = (me < 2) | (me >= 6)

    @pl.when(is_owner)
    def _():
        for step in range(1, 8):
            greet((me + step) % 8)

    pl.semaphore_wait(pltpu.get_barrier_semaphore(), 4 - is_owner.astype(jnp.int32))
    rows = pl.ds(pl.multiple_of(me * 32, 32), 32)

    for block, owner in enumerate(OWNERS):
        for orbital in range(2):
            source = own.at[orbital, block]
            target = out.at[orbital, :, rows]

            @pl.when(me != owner)
            def _(source=source, target=target, block=block, orbital=orbital, owner=owner):
                remote(
                    source, target, send_sem.at[orbital, block], recv_sem.at[orbital, me], owner
                ).start()

            @pl.when(me == owner)
            def _(source=source, target=target, orbital=orbital):
                pltpu.make_async_copy(source, target, local_sem.at[orbital]).start()

    for block, owner in enumerate(OWNERS):
        for orbital in range(2):
            source = own.at[orbital, block]
            target = out.at[orbital, :, rows]

            @pl.when(me != owner)
            def _(source=source, target=target, block=block, orbital=orbital, owner=owner):
                remote(
                    source, target, send_sem.at[orbital, block], recv_sem.at[orbital, me], owner
                ).wait_send()

            @pl.when(me == owner)
            def _(source=source, target=target, orbital=orbital):
                pltpu.make_async_copy(source, target, local_sem.at[orbital]).wait()

    @pl.when(is_owner)
    def _():
        for step in range(1, 8):
            sender = (me + step) % 8
            for orbital in range(2):
                theirs = out.at[orbital, :, pl.ds(pl.multiple_of(sender * 32, 32), 32)]
                remote(
                    own.at[orbital, 0],
                    theirs,
                    send_sem.at[orbital, 0],
                    recv_sem.at[orbital, sender],
                    sender,
                ).wait_recv()


def collect(own):
    return pl.pallas_call(
        collect_kernel,
        out_shape=jax.ShapeDtypeStruct((2, 32, 256, 128), jnp.bfloat16),
        in_specs=[pl.BlockSpec(memory_space=pl.ANY)],
        out_specs=pl.BlockSpec(memory_space=pl.ANY),
        scratch_shapes=[
            pltpu.SemaphoreType.DMA((2,)),
            pltpu.SemaphoreType.DMA((2, 4)),
            pltpu.SemaphoreType.DMA((2, 8)),
        ],
        compiler_params=pltpu.CompilerParams(collective_id=2, has_side_effects=True),
        name="collect",
    )(own)


def matmul(left, right):
    return jnp.dot(left, right, preferred_element_type=jnp.float32)


def swap(value):
    return jnp.transpose(value, (1, 0, 2))


def grid_kernel(
    place, count, rows, table_y, table_z, proj, atom, real, sums, cells, patches
):
    def plane(x, carry):
        second = matmul(table_y[...], rows[0, x]).astype(jnp.bfloat16)
        value = matmul(second, table_z[...]).astype(jnp.bfloat16)
        real[0, x] = value
        wide = value.astype(jnp.float32)
        base = pl.multiple_of(x * 512, 512)
        cells[pl.ds(base, 256), :] = wide[:, :128]
        cells[pl.ds(base + 256, 256), :] = wide[:, 128:]
        return carry

    lax.fori_loop(0, 32, plane, 0, unroll=4)

    def fetch(group, carry):
        base = pl.multiple_of(group * 8, 8)
        for k in range(8):
            patches[pl.ds(base + k, 1), :] = cells[pl.ds(place[base + k], 1), :]
        return carry

    lax.fori_loop(0, 64, fetch, 0)
    high = lax.Precision.HIGHEST
    atoms = lax.broadcasted_iota(jnp.int32, (128, 512), 0)
    slots = lax.broadcasted_iota(jnp.int32, (128, 512), 1)
    chosen = ((atoms == atom[...]) & (slots < count[0])).astype(jnp.float32)
    ones = jnp.ones((8, 128), jnp.float32)
    for p in range(4):
        product = patches[...] * proj[p].astype(jnp.float32)
        by_atom = jnp.dot(chosen, product, precision=high, preferred_element_type=jnp.float32)
        summed = lax.dot_general(
            ones, by_atom, (((1,), (1,)), ((), ())), precision=high, preferred_element_type=jnp.float32
        )
        sums[0, p : p + 1, :] = summed[0:1]


def whole(shape):
    return pl.BlockSpec(shape, lambda *_: (0,) * len(shape), pipeline_mode=pl.Buffered(1))


def to_grid(place, count, rows, table_y, table_z, proj, atom):
    smem = pl.BlockSpec(memory_space=pltpu.SMEM)
    return pl.pallas_call(
        grid_kernel,
        grid=(2,),
        out_shape=(
            jax.ShapeDtypeStruct((2, 32, 256, 256), jnp.bfloat16),
            jax.ShapeDtypeStruct((2, 4, 128), jnp.float32),
        ),
        in_specs=[
            smem,
            smem,
            pl.BlockSpec((1, 32, 128, 128), lambda o: (o, 0, 0, 0)),
            whole((256, 128)),
            whole((128, 256)),
            whole((4, 512, 128)),
            whole((1, 512)),
        ],
        out_specs=(
            pl.BlockSpec((1, 32, 256, 256), lambda o: (o, 0, 0, 0)),
            pl.BlockSpec((1, 4, 128), lambda o: (o, 0, 0)),
        ),
        scratch_shapes=[
            pltpu.VMEM((16384, 128), jnp.float32),
            pltpu.VMEM((512, 128), jnp.float32),
        ],
        compiler_params=pltpu.CompilerParams(vmem_limit_bytes=VMEM_BYTES),
        name="to_grid",
    )(place, count, rows, table_y, table_z, proj, atom)


def product_kernel(
    place, count, real, potential, weights, proj, atom, table_z, table_y, out, cells, added, fourth
):
    def multiply(x, carry):
        value = potential[x] * real[0, x].astype(jnp.float32)
        base = pl.multiple_of(x * 512, 512)
        cells[pl.ds(base, 256), :] = value[:, :128]
        cells[pl.ds(base + 256, 256), :] = value[:, 128:]
        return carry

    lax.fori_loop(0, 32, multiply, 0, unroll=2)
    atoms = lax.broadcasted_iota(jnp.int32, (512, 128), 1)
    slots = lax.broadcasted_iota(jnp.int32, (512, 128), 0)
    chosen = ((atoms == atom[...]) & (slots < count[0])).astype(jnp.float32)
    strength = jnp.concatenate([weights[0], weights[0]], axis=0)
    back = lax.dot_general(
        chosen,
        strength,
        (((1,), (1,)), ((), ())),
        precision=lax.Precision.HIGHEST,
        preferred_element_type=jnp.float32,
    )
    patch = back[:, 0:1] * proj[0].astype(jnp.float32)
    for p in range(1, 4):
        patch = patch + back[:, p : p + 1] * proj[p].astype(jnp.float32)
    added[...] = patch

    def store(group, carry):
        base = pl.multiple_of(group * 8, 8)
        for k in range(8):
            row = pl.ds(place[base + k], 1)
            cells[row, :] = cells[row, :] + added[pl.ds(base + k, 1), :]
        return carry

    lax.fori_loop(0, 64, store, 0)

    def plane(x, carry):
        base = pl.multiple_of(x * 512, 512)
        low = cells[pl.ds(base, 256), :].astype(jnp.bfloat16)
        top = cells[pl.ds(base + 256, 256), :].astype(jnp.bfloat16)
        third = matmul(jnp.concatenate([low, top], axis=1), table_z[...]).astype(jnp.bfloat16)
        fourth[x] = matmul(table_y[...], third)
        return carry

    lax.fori_loop(0, 32, plane, 0, unroll=4)

    def turn(group, carry):
        block, inner = group // 4, group % 4
        value = fourth[:, pl.ds(pl.multiple_of(group * 8, 8), 8), :]
        out[0, block, pl.ds(inner * 8, 8)] = swap(value).astype(jnp.bfloat16)
        return carry

    lax.fori_loop(0, 16, turn, 0)


def from_grid(place, count, real, potential, weights, proj, atom, table_z, table_y):
    smem = pl.BlockSpec(memory_space=pltpu.SMEM)
    return pl.pallas_call(
        product_kernel,
        grid=(2,),
        out_shape=jax.ShapeDtypeStruct((2, 4, 32, 32, 128), jnp.bfloat16),
        in_specs=[
            smem,
            smem,
            pl.BlockSpec((1, 32, 256, 256), lambda o: (o, 0, 0, 0)),
            whole((32, 256, 256)),
            pl.BlockSpec((1, 4, 128), lambda o: (o, 0, 0)),
            whole((4, 512, 128)),
            whole((512, 1)),
            whole((256, 128)),
            whole((128, 256)),
        ],
        out_specs=pl.BlockSpec((1, 4, 32, 32, 128), lambda o: (o, 0, 0, 0, 0)),
        scratch_shapes=[
            pltpu.VMEM((16384, 128), jnp.float32),
            pltpu.VMEM((512, 128), jnp.float32),
            pltpu.VMEM((32, 128, 128), jnp.float32),
        ],
        compiler_params=pltpu.CompilerParams(vmem_limit_bytes=VMEM_BYTES),
        name="from_grid",
    )(place, count, real, potential, weights, proj, atom, table_z, table_y)


def last_kernel(index, rows, table_x, coeff, sphere, out):
    block, orbital = pl.program_id(0), pl.program_id(1)
    shard = index[0]
    used = ((block < 2) | (block >= 6)) & ((shard < 2) | (shard >= 6))

    @pl.when(jnp.logical_not(used))
    def _():
        out[...] = jnp.zeros_like(out)

    def squares(start, shape, axis):
        at = lax.broadcasted_iota(jnp.int32, shape, axis) + start
        return (frequency(at, 256).astype(jnp.float32) * (4.0 / 256)) ** 2

    @pl.when(used)
    def _():
        table = table_x[...]
        for group in range(2):
            here = slice(group * 16, group * 16 + 16)
            found = [matmul(table, rows[orbital, group * 16 + k]) for k in range(16)]
            spectrum = swap(jnp.stack(found))
            kin_xy = squares(block * 32, (32, 16, 128), 0) + squares(
                shard * 32 + group * 16, (32, 16, 128), 1
            )
            for half in range(2):
                lanes = slice(half * 128, half * 128 + 128)
                ball = sphere[:, here, lanes].astype(jnp.float32)
                masked = coeff[0, :, here, lanes].astype(jnp.float32) * ball
                kinetic = 2.0 * (kin_xy + squares(half * 128, (32, 16, 128), 2))
                result = ball * (spectrum + kinetic * masked)
                out[0, :, here, lanes] = result.astype(jnp.bfloat16)


def last(index, rows, table_x, coeff, sphere):
    def used_block(b):
        return jnp.where((b >= 2) & (b < 6), 1, b)

    return pl.pallas_call(
        last_kernel,
        grid=(8, 2),
        out_shape=jax.ShapeDtypeStruct(coeff.shape, jnp.bfloat16),
        in_specs=[
            pl.BlockSpec(memory_space=pltpu.SMEM),
            whole((2, 32, 256, 128)),
            pl.BlockSpec((32, 256), lambda b, o: (used_block(b), 0)),
            pl.BlockSpec((1, 32, 32, 256), lambda b, o: (o, used_block(b), 0, 0)),
            pl.BlockSpec((32, 32, 256), lambda b, o: (used_block(b), 0, 0)),
        ],
        out_specs=pl.BlockSpec((1, 32, 32, 256), lambda b, o: (o, b, 0, 0)),
        compiler_params=pltpu.CompilerParams(vmem_limit_bytes=VMEM_BYTES),
        name="last",
    )(index, rows, table_x, coeff, sphere)


def used_rows(table):
    return jnp.concatenate([table[:64], table[192:]], axis=0)


def line_of_chips(coeff, sphere, potential, proj_values, tile_cell, tile_atom, tile_count, dion):
    own_index = lax.axis_index("fft")
    table = cas_table(256)
    part = used_rows(table)
    is_owner = ((own_index < 2) | (own_index >= 6)).astype(jnp.int32)[None]
    proj = lax.all_gather(proj_values, "band", axis=2, tiled=True).transpose(1, 0, 2)
    place = tile_cell // 512 * 512 + tile_cell % 2 * 256 + tile_cell % 512 // 2
    rows = spread(sections(is_owner, coeff, sphere, part.T))
    real, sums = to_grid(place, tile_count, rows, part.T, part, proj, tile_atom[None, :])
    weights = total(sums, jnp.broadcast_to(dion[None, :, None], sums.shape))
    fourth = from_grid(
        place, tile_count, real, potential, weights, proj, tile_atom[:, None], part.T, part
    )
    return last(own_index[None], collect(fourth), table, coeff, sphere)


def local(*values):
    coeff, slots, shards = values[0], values[4].shape[0], lax.axis_size("fft")
    if coeff.shape == (2, 256, 32, 256) and shards == 8 and slots == 512:
        return line_of_chips(*values)
    return general(*values)


def solution(mesh):
    in_specs = (
        P("band", None, "fft", None),
        P(None, "fft", None),
        P("fft", None, None),
        P("fft", None, "band"),
        P("fft"),
        P("fft"),
        P("fft"),
        P(),
    )
    out_specs = P("band", None, "fft", None)
    return jax.shard_map(local, mesh=mesh, in_specs=in_specs, out_specs=out_specs, check_vma=False)
```

```python
import math

import jax
import jax.numpy as jnp
from jax import lax
from jax.experimental import pallas as pl
from jax.experimental.pallas import tpu as pltpu
from jax.sharding import PartitionSpec as P

APD = 16
REACH = 3
MESH = pl.DeviceIdType.MESH
VMEM_BYTES = 58 * 2**20


def from_behind(value, axis, steps):
    count = lax.axis_size(axis)
    pairs = [(source, (source + steps) % count) for source in range(count)]
    return lax.ppermute(value, axis, pairs)


def cas_table(length):
    index = jnp.arange(length, dtype=jnp.int32)
    product = index[:, None] * index[None, :] % length
    angle = product.astype(jnp.float32) * (2.0 * math.pi / length)
    return ((jnp.cos(angle) + jnp.sin(angle)) * (1.0 / math.sqrt(length))).astype(jnp.bfloat16)


def frequency(index, length):
    return jnp.minimum(index, length - index)


def general(coeff, sphere, potential, proj_values, tile_cell, tile_atom, tile_count, dion):
    high = lax.Precision.HIGHEST
    orbitals, full_x, local_y, full_z = coeff.shape
    shards = lax.axis_size("fft")
    own_index = lax.axis_index("fft")
    full_y = local_y * shards
    table_x = cas_table(full_x)
    table_y = cas_table(full_y)
    table_z = cas_table(full_z)
    sphere_real = sphere.astype(jnp.float32)
    masked = (coeff.astype(jnp.float32) * sphere_real[None]).astype(jnp.bfloat16)
    row_x = frequency(jnp.arange(full_x, dtype=jnp.int32), full_x).astype(jnp.float32)
    row_y = frequency(own_index * local_y + jnp.arange(local_y, dtype=jnp.int32), full_y).astype(
        jnp.float32
    )
    row_z = frequency(jnp.arange(full_z, dtype=jnp.int32), full_z).astype(jnp.float32)
    kinetic = 2.0 * (
        (4.0 * row_x / full_x)[:, None, None] ** 2
        + (4.0 * row_y / full_y)[None, :, None] ** 2
        + (4.0 * row_z / full_z)[None, None, :] ** 2
    )
    section_one = jnp.einsum(
        "ax,oxyz->oayz", table_x, masked, preferred_element_type=jnp.float32
    ).astype(jnp.bfloat16)
    along_y = jnp.einsum(
        "by,oxyz->oxbz",
        table_y,
        lax.all_to_all(section_one, "fft", split_axis=1, concat_axis=2, tiled=True),
        preferred_element_type=jnp.float32,
    ).astype(jnp.bfloat16)
    real = jnp.dot(along_y, table_z, preferred_element_type=jnp.float32).astype(jnp.bfloat16)
    whole_proj = lax.all_gather(proj_values, "band", axis=2, tiled=True)
    flat = real.reshape(orbitals, -1, 128)
    patches = jnp.take(flat, tile_cell, axis=1)
    slots = tile_cell.shape[0]
    live = (jnp.arange(slots, dtype=jnp.int32) < tile_count[0]).astype(jnp.float32)
    partial_value = (
        jnp.einsum("otc,tpc->otp", patches, whole_proj, preferred_element_type=jnp.float32)
        * live[None, :, None]
    )
    width = (2 * REACH + 1) * APD
    home = tile_atom // APD
    local_atom = (home - own_index + REACH) % shards * APD + tile_atom % APD
    onehot = (local_atom[:, None] == jnp.arange(width, dtype=jnp.int32)[None, :]).astype(
        jnp.float32
    )
    table = jnp.einsum("otp,ta->oap", partial_value, onehot, precision=high)
    intersection = table
    for offset in range(-2 * REACH, 2 * REACH + 1):
        if offset != 0:
            arrived = from_behind(table, "fft", offset)
            first = max(0, -offset)
            last = min(2 * REACH, 2 * REACH - offset)
            intersection = intersection.at[:, first * APD : (last + 1) * APD].add(
                arrived[:, (first + offset) * APD : (last + offset + 1) * APD]
            )
    weights = intersection * dion[None, None, :]
    back = jnp.einsum("oap,ta->otp", weights, onehot, precision=high) * live[None, :, None]
    added = jnp.einsum("otp,tpc->otc", back, whole_proj.astype(jnp.float32), precision=high)
    nonlocal_part = (
        jnp.zeros(flat.shape, jnp.float32).at[:, tile_cell].add(added).reshape(real.shape)
    )
    mixed = (potential[None] * real.astype(jnp.float32) + nonlocal_part).astype(jnp.bfloat16)
    section_three = jnp.dot(mixed, table_z, preferred_element_type=jnp.float32).astype(jnp.bfloat16)
    section_four = jnp.einsum(
        "by,oxyz->oxbz", table_y, section_three, preferred_element_type=jnp.float32
    ).astype(jnp.bfloat16)
    spectrum = jnp.einsum(
        "ax,oxyz->oayz",
        table_x,
        lax.all_to_all(section_four, "fft", split_axis=2, concat_axis=1, tiled=True),
        preferred_element_type=jnp.float32,
    )
    result = sphere_real[None] * (spectrum + kinetic[None] * masked.astype(jnp.float32))
    return result.astype(jnp.bfloat16)


def remote(source, target, send_sem, recv_sem, device, axis="fft"):
    return pltpu.make_async_remote_copy(
        src_ref=source,
        dst_ref=target,
        send_sem=send_sem,
        recv_sem=recv_sem,
        device_id={axis: device},
        device_id_type=MESH,
    )


def greet(device, axis="fft"):
    pl.semaphore_signal(
        pltpu.get_barrier_semaphore(), inc=1, device_id={axis: device}, device_id_type=MESH
    )


OWNERS = (0, 1, 6, 7)
HIGH = lax.Precision.HIGHEST


def matmul(left, right):
    return jnp.dot(left, right, preferred_element_type=jnp.float32)


def exact(left, right, dims=((1,), (0,))):
    return lax.dot_general(
        left, right, (dims, ((), ())), precision=HIGH, preferred_element_type=jnp.float32
    )


def swap(value):
    return jnp.transpose(value, (1, 0, 2))


def slab(at):
    return pl.ds(pl.multiple_of(at * 32, 32), 32)


def kernel(
    cell, count, dion, cell_row, atom_row, own_proj, table_in, table_out, coeff, sphere, potential,
    out,
    waves, ball, field, first, rows, cells, proj_parts, proj, spots, patches, high_part, low_part,
    planes_of, slot_atom, tables, fourth, back, gathered, ready, empty,
    load_sem, zero_sem, out_sem, proj_send, proj_recv, first_send, first_recv, table_send, table_recv,
    back_send, back_recv, keep_sem,
):
    me, band = lax.axis_index("fft"), lax.axis_index("band")
    is_owner = (me < 2) | (me >= 6)
    own_block = jnp.where(me < 2, me, me - 4)

    def load_waves(orbital, half):
        return pltpu.make_async_copy(
            coeff.at[orbital, pl.ds(half * 192, 64)],
            waves.at[orbital, pl.ds(half * 64, 64)],
            load_sem.at[orbital, half],
        )

    def load_ball(half):
        return pltpu.make_async_copy(
            sphere.at[pl.ds(half * 192, 64)], ball.at[pl.ds(half * 64, 64)], load_sem.at[2, half]
        )

    load_field = pltpu.make_async_copy(potential, field, load_sem.at[3, 0])

    def clear(step):
        return pltpu.make_async_copy(
            empty, out.at[step // 8, slab(step % 8)], zero_sem.at[step // 8, step % 8]
        )

    def cleared(act):
        def one(step, carry):
            at = step % 8

            @pl.when(jnp.logical_not(is_owner) | ((at >= 2) & (at < 6)))
            def _():
                act(clear(step))

            return carry

        lax.fori_loop(0, 16, one, 0)

    @pl.when(is_owner)
    def _():
        for half in range(2):
            load_ball(half).start()
            load_waves(0, half).start()
        for half in range(2):
            load_waves(1, half).start()

    for step in range(1, 8):
        greet((me + step) % 8)
    for step in range(1, 4):
        greet((band + step) % 4, "band")
    pl.semaphore_wait(pltpu.get_barrier_semaphore(), 10)

    def send_proj(step):
        return remote(
            own_proj,
            proj_parts.at[band],
            proj_send.at[step],
            proj_recv.at[step],
            (band + step) % 4,
            "band",
        )

    for step in range(1, 4):
        send_proj(step).start()

    def slot(orbital, at):
        return rows.at[orbital, :, slab(at)]

    def send_first(orbital, step):
        there = (me + step) % 8
        return remote(
            first.at[orbital, slab(there)],
            slot(orbital, own_block),
            first_send.at[orbital, step],
            first_recv.at[orbital, own_block],
            there,
        )

    def keep_first(orbital):
        return pltpu.make_async_copy(
            first.at[orbital, slab(me)], slot(orbital, own_block), keep_sem.at[0, orbital]
        )

    def section(orbital, carry):
        near = lax.broadcasted_iota(jnp.int32, (64, 32, 128), 2) < 64
        for half in range(2):
            load_waves(orbital, half).wait()
            part = pl.ds(half * 64, 64)
            value = waves[orbital, part].astype(jnp.float32) * ball[part].astype(jnp.float32)
            value = jnp.where(near, value[..., :128], value[..., 128:])
            spots[:, part, :] = swap(value).astype(jnp.bfloat16)

        def along_x(block, inner):
            part = pl.ds(pl.multiple_of(block * 64, 64), 64)
            table = table_in[part, :]
            for group in range(2):
                found = [matmul(table, spots[group * 16 + k]) for k in range(16)]
                value = swap(jnp.stack(found)).astype(jnp.bfloat16)
                first[orbital, part, group * 16 : group * 16 + 16, :] = value
            return inner

        lax.fori_loop(0, 4, along_x, 0)
        for step in range(1, 8):
            send_first(orbital, step).start()
        keep_first(orbital).start()
        return carry

    @pl.when(is_owner)
    def _():
        for half in range(2):
            load_ball(half).wait()
        lax.fori_loop(0, 2, section, 0)

    load_field.start()
    empty[...] = jnp.zeros_like(empty)
    cleared(lambda copy: copy.start())

    cells_at = cell_row[...]
    in_plane = (cells_at & 1) * 256 + ((cells_at & 511) >> 1)
    at_row = lax.broadcasted_iota(jnp.int32, (512, 512), 0)
    patches_at = (at_row == in_plane).astype(jnp.float32)
    tables_row = patches_at.astype(jnp.bfloat16)
    planes_row = jnp.broadcast_to((cells_at >> 9).astype(jnp.float32), (128, 512))
    planes_of[...] = jnp.transpose(planes_row, (1, 0))
    atoms = lax.broadcasted_iota(jnp.int32, (128, 512), 0)
    slots = lax.broadcasted_iota(jnp.int32, (128, 512), 1)
    chosen = ((atoms == atom_row[...]) & (slots < count[0])).astype(jnp.float32)
    slot_atom[...] = jnp.transpose(chosen, (1, 0))
    proj_parts[band] = own_proj[...]
    for step in range(1, 4):
        source = proj_parts.at[(band + 4 - step) % 4]
        copy = remote(
            own_proj, source, proj_send.at[step], proj_recv.at[step], (band + step) % 4, "band"
        )
        copy.wait_recv()
        copy.wait_send()
    lane_in = lax.broadcasted_iota(jnp.int32, (128, 128), 0)
    lane_out = lax.broadcasted_iota(jnp.int32, (128, 128), 1)
    for p in range(4):
        whole = jnp.zeros((512, 128), jnp.float32)
        for part in range(4):
            wanted = (lane_in == lane_out + 32 * (p - part)) & (lane_out // 32 == part)
            move = wanted.astype(jnp.float32).astype(jnp.bfloat16)
            whole = whole + matmul(proj_parts[part], move)
        proj[p] = whole
    load_field.wait()

    def send_table(orbital, step):
        return remote(
            tables.at[orbital, me],
            tables.at[orbital, me],
            table_send.at[orbital, step],
            table_recv.at[orbital, step],
            (me + step) % 8,
        )

    def send_back(orbital, block, owner):
        return remote(
            back.at[orbital, block],
            gathered.at[orbital, :, slab(me)],
            back_send.at[orbital, block],
            back_recv.at[orbital, me],
            owner,
        )

    def keep_back(orbital, block):
        return pltpu.make_async_copy(
            back.at[orbital, block], gathered.at[orbital, :, slab(me)], keep_sem.at[1, orbital]
        )

    def one_orbital(orbital, carry):
        for at, owner in enumerate(OWNERS):

            @pl.when(me != owner)
            def _(at=at, owner=owner):
                remote(
                    first.at[orbital, slab(0)],
                    slot(orbital, at),
                    first_send.at[orbital, 0],
                    first_recv.at[orbital, at],
                    owner,
                ).wait_recv()

        @pl.when(is_owner)
        def _():
            keep_first(orbital).wait()

        def to_plane(x, inner):
            second = matmul(table_in[...], rows[orbital, x]).astype(jnp.bfloat16)
            wide = matmul(second, table_out[...]).astype(jnp.bfloat16).astype(jnp.float32)
            base = pl.multiple_of(x * 512, 512)
            cells[pl.ds(base, 256), :] = wide[:, :128]
            cells[pl.ds(base + 256, 256), :] = wide[:, 128:]
            return inner

        lax.fori_loop(0, 32, to_plane, 0, unroll=4)

        def fetch(group, inner):
            base = pl.multiple_of(group * 8, 8)
            for k in range(8):
                at = cell[base + k]
                row = (at >> 9) * 512 + (at & 1) * 256 + ((at & 511) >> 1)
                patches[pl.ds(base + k, 1), :] = cells[pl.ds(row, 1), :]
            return inner

        lax.fori_loop(0, 64, fetch, 0)
        of_slot = slot_atom[...]
        ones = jnp.ones((8, 128), jnp.float32)
        for p in range(4):
            by_atom = exact(chosen, patches[...] * proj[p])
            tables[orbital, me, p : p + 1, :] = exact(ones, by_atom, ((1,), (1,)))[0:1]
        for step in range(1, 8):
            send_table(orbital, step).start()
        for step in range(1, 8):
            source = tables.at[orbital, (me + 8 - step) % 8]
            copy = remote(
                source,
                source,
                table_send.at[orbital, step],
                table_recv.at[orbital, step],
                (me + step) % 8,
            )
            copy.wait_recv()
            copy.wait_send()
        total = tables[orbital, 0]
        for other in range(1, 8):
            total = total + tables[orbital, other]
        strength = exact(of_slot, jnp.concatenate([total, total], axis=0), ((1,), (1,)))
        added = strength[:, 0:1] * dion[0] * proj[0]
        for p in range(1, 4):
            added = added + strength[:, p : p + 1] * dion[p] * proj[p]
        top = added.astype(jnp.bfloat16).astype(jnp.float32)
        high_part[...] = top
        low_part[...] = added - top

        def from_plane(x, inner):
            here = planes_of[...] == x.astype(jnp.float32)
            pieces = jnp.concatenate(
                [
                    jnp.where(here, high_part[...], 0.0).astype(jnp.bfloat16),
                    jnp.where(here, low_part[...], 0.0).astype(jnp.bfloat16),
                ],
                axis=1,
            )
            spread = matmul(tables_row, pieces)
            spread = spread[:, :128] + spread[:, 128:]
            base = pl.multiple_of(x * 512, 512)
            level = field[x]
            left = level[:, :128] * cells[pl.ds(base, 256), :] + spread[:256]
            right = level[:, 128:] * cells[pl.ds(base + 256, 256), :] + spread[256:]
            mixed = jnp.concatenate([left.astype(jnp.bfloat16), right.astype(jnp.bfloat16)], axis=1)
            third = matmul(mixed, table_in[...]).astype(jnp.bfloat16)
            fourth[x] = matmul(table_out[...], third)
            return inner

        lax.fori_loop(0, 32, from_plane, 0, unroll=2)

        def turn(group, inner):
            value = fourth[:, pl.ds(pl.multiple_of(group * 8, 8), 8), :]
            back[orbital, group // 4, pl.ds(group % 4 * 8, 8)] = swap(value).astype(jnp.bfloat16)
            return inner

        lax.fori_loop(0, 16, turn, 0)
        for block, owner in enumerate(OWNERS):

            @pl.when(me != owner)
            def _(block=block, owner=owner):
                send_back(orbital, block, owner).start()

            @pl.when(me == owner)
            def _(block=block):
                keep_back(orbital, block).start()

        return carry

    lax.fori_loop(0, 2, one_orbital, 0)

    def squares(start, shape, axis):
        at = lax.broadcasted_iota(jnp.int32, shape, axis) + start
        return (frequency(at, 256).astype(jnp.float32) * (4.0 / 256)) ** 2

    def write(step):
        orbital, block = step // 4, step % 4
        at = block + block // 2 * 4
        return pltpu.make_async_copy(
            ready.at[step % 2], out.at[orbital, slab(at)], out_sem.at[step % 2]
        )

    def finish(step, carry):
        orbital, block = step // 4, step % 4

        @pl.when(block == 0)
        def _():
            for other in range(1, 8):
                sender = (me + other) % 8
                remote(
                    back.at[orbital, 0],
                    gathered.at[orbital, :, slab(sender)],
                    back_send.at[orbital, 0],
                    back_recv.at[orbital, sender],
                    sender,
                ).wait_recv()
            keep_back(orbital, own_block).wait()

        @pl.when(step >= 2)
        def _():
            write(step - 2).wait()

        table = table_out[slab(block), :]
        start = block * 32 + block // 2 * 128
        for group in range(2):
            here = slice(group * 16, group * 16 + 16)
            found = [matmul(table, gathered[orbital, group * 16 + k]) for k in range(16)]
            spectrum = swap(jnp.stack(found))
            kin_xy = squares(start, (32, 16, 128), 0) + squares(
                me * 32 + group * 16, (32, 16, 128), 1
            )
            for half in range(2):
                lanes = slice(half * 128, half * 128 + 128)
                inside = ball[slab(block), here, lanes].astype(jnp.float32)
                masked = waves[orbital, slab(block), here, lanes].astype(jnp.float32) * inside
                kinetic = 2.0 * (kin_xy + squares(half * 128, (32, 16, 128), 2))
                result = inside * (spectrum + kinetic * masked)
                ready[step % 2, :, here, lanes] = result.astype(jnp.bfloat16)
        write(step).start()
        return carry

    @pl.when(is_owner)
    def _():
        lax.fori_loop(0, 8, finish, 0)
        write(6).wait()
        write(7).wait()
        for orbital in range(2):
            for step in range(1, 8):
                send_first(orbital, step).wait_send()

    for orbital in range(2):
        for block, owner in enumerate(OWNERS):

            @pl.when(me != owner)
            def _(orbital=orbital, block=block, owner=owner):
                send_back(orbital, block, owner).wait_send()

    cleared(lambda copy: copy.wait())


def line_of_chips(coeff, sphere, potential, proj_values, tile_cell, tile_atom, tile_count, dion):
    table = cas_table(256)
    table_out = jnp.concatenate([table[:64], table[192:]], axis=0)
    smem = pl.BlockSpec(memory_space=pltpu.SMEM)
    vmem = pl.BlockSpec(memory_space=pltpu.VMEM)
    anywhere = pl.BlockSpec(memory_space=pl.ANY)
    dma = pltpu.SemaphoreType.DMA
    half, single = jnp.bfloat16, jnp.float32
    return pl.pallas_call(
        kernel,
        out_shape=jax.ShapeDtypeStruct(coeff.shape, half),
        in_specs=[smem] * 3 + [vmem] * 5 + [anywhere] * 3,
        out_specs=anywhere,
        scratch_shapes=[
            pltpu.VMEM((2, 128, 32, 256), half),
            pltpu.VMEM((128, 32, 256), jnp.int32),
            pltpu.VMEM((32, 256, 256), single),
            pltpu.VMEM((2, 256, 32, 128), half),
            pltpu.VMEM((2, 32, 128, 128), half),
            pltpu.VMEM((16384, 128), single),
            pltpu.VMEM((4, 512, 128), half),
            pltpu.VMEM((4, 512, 128), single),
            pltpu.VMEM((32, 128, 128), half),
            pltpu.VMEM((512, 128), single),
            pltpu.VMEM((512, 128), single),
            pltpu.VMEM((512, 128), single),
            pltpu.VMEM((512, 128), single),
            pltpu.VMEM((512, 128), single),
            pltpu.VMEM((2, 8, 4, 128), single),
            pltpu.VMEM((32, 128, 128), single),
            pltpu.VMEM((2, 4, 32, 32, 128), half),
            pltpu.VMEM((2, 32, 256, 128), half),
            pltpu.VMEM((2, 32, 32, 256), half),
            pltpu.VMEM((32, 32, 256), half),
            dma((4, 2)),
            dma((2, 8)),
            dma((2,)),
            dma((4,)),
            dma((4,)),
            dma((2, 8)),
            dma((2, 4)),
            dma((2, 8)),
            dma((2, 8)),
            dma((2, 4)),
            dma((2, 8)),
            dma((2, 2)),
        ],
        compiler_params=pltpu.CompilerParams(
            collective_id=0, has_side_effects=True, vmem_limit_bytes=VMEM_BYTES
        ),
        name="hamiltonian",
    )(
        tile_cell,
        tile_count,
        dion,
        tile_cell[None, :],
        tile_atom[None, :],
        proj_values.reshape(512, 128),
        table_out.T,
        table_out,
        coeff,
        sphere,
        potential,
    )


def local(*values):
    coeff, slots, shards = values[0], values[4].shape[0], lax.axis_size("fft")
    if coeff.shape == (2, 256, 32, 256) and shards == 8 and slots == 512:
        return line_of_chips(*values)
    return general(*values)


def solution(mesh):
    in_specs = (
        P("band", None, "fft", None),
        P(None, "fft", None),
        P("fft", None, None),
        P("fft", None, "band"),
        P("fft"),
        P("fft"),
        P("fft"),
        P(),
    )
    out_specs = P("band", None, "fft", None)
    return jax.shard_map(local, mesh=mesh, in_specs=in_specs, out_specs=out_specs, check_vma=False)
```

```python
import math

import jax
import jax.numpy as jnp
from jax import lax
from jax.experimental import pallas as pl
from jax.experimental.pallas import tpu as pltpu
from jax.sharding import PartitionSpec as P

APD = 16
REACH = 3
MESH = pl.DeviceIdType.MESH
VMEM_BYTES = 58 * 2**20


def from_behind(value, axis, steps):
    count = lax.axis_size(axis)
    pairs = [(source, (source + steps) % count) for source in range(count)]
    return lax.ppermute(value, axis, pairs)


def cas_table(length):
    index = jnp.arange(length, dtype=jnp.int32)
    product = index[:, None] * index[None, :] % length
    angle = product.astype(jnp.float32) * (2.0 * math.pi / length)
    return ((jnp.cos(angle) + jnp.sin(angle)) * (1.0 / math.sqrt(length))).astype(jnp.bfloat16)


def frequency(index, length):
    return jnp.minimum(index, length - index)


def general(coeff, sphere, potential, proj_values, tile_cell, tile_atom, tile_count, dion):
    high = lax.Precision.HIGHEST
    orbitals, full_x, local_y, full_z = coeff.shape
    shards = lax.axis_size("fft")
    own_index = lax.axis_index("fft")
    full_y = local_y * shards
    table_x = cas_table(full_x)
    table_y = cas_table(full_y)
    table_z = cas_table(full_z)
    sphere_real = sphere.astype(jnp.float32)
    masked = (coeff.astype(jnp.float32) * sphere_real[None]).astype(jnp.bfloat16)
    row_x = frequency(jnp.arange(full_x, dtype=jnp.int32), full_x).astype(jnp.float32)
    row_y = frequency(own_index * local_y + jnp.arange(local_y, dtype=jnp.int32), full_y).astype(
        jnp.float32
    )
    row_z = frequency(jnp.arange(full_z, dtype=jnp.int32), full_z).astype(jnp.float32)
    kinetic = 2.0 * (
        (4.0 * row_x / full_x)[:, None, None] ** 2
        + (4.0 * row_y / full_y)[None, :, None] ** 2
        + (4.0 * row_z / full_z)[None, None, :] ** 2
    )
    section_one = jnp.einsum(
        "ax,oxyz->oayz", table_x, masked, preferred_element_type=jnp.float32
    ).astype(jnp.bfloat16)
    along_y = jnp.einsum(
        "by,oxyz->oxbz",
        table_y,
        lax.all_to_all(section_one, "fft", split_axis=1, concat_axis=2, tiled=True),
        preferred_element_type=jnp.float32,
    ).astype(jnp.bfloat16)
    real = jnp.dot(along_y, table_z, preferred_element_type=jnp.float32).astype(jnp.bfloat16)
    whole_proj = lax.all_gather(proj_values, "band", axis=2, tiled=True)
    flat = real.reshape(orbitals, -1, 128)
    patches = jnp.take(flat, tile_cell, axis=1)
    slots = tile_cell.shape[0]
    live = (jnp.arange(slots, dtype=jnp.int32) < tile_count[0]).astype(jnp.float32)
    partial_value = (
        jnp.einsum("otc,tpc->otp", patches, whole_proj, preferred_element_type=jnp.float32)
        * live[None, :, None]
    )
    width = (2 * REACH + 1) * APD
    home = tile_atom // APD
    local_atom = (home - own_index + REACH) % shards * APD + tile_atom % APD
    onehot = (local_atom[:, None] == jnp.arange(width, dtype=jnp.int32)[None, :]).astype(
        jnp.float32
    )
    table = jnp.einsum("otp,ta->oap", partial_value, onehot, precision=high)
    intersection = table
    for offset in range(-2 * REACH, 2 * REACH + 1):
        if offset != 0:
            arrived = from_behind(table, "fft", offset)
            first = max(0, -offset)
            last = min(2 * REACH, 2 * REACH - offset)
            intersection = intersection.at[:, first * APD : (last + 1) * APD].add(
                arrived[:, (first + offset) * APD : (last + offset + 1) * APD]
            )
    weights = intersection * dion[None, None, :]
    back = jnp.einsum("oap,ta->otp", weights, onehot, precision=high) * live[None, :, None]
    added = jnp.einsum("otp,tpc->otc", back, whole_proj.astype(jnp.float32), precision=high)
    nonlocal_part = (
        jnp.zeros(flat.shape, jnp.float32).at[:, tile_cell].add(added).reshape(real.shape)
    )
    mixed = (potential[None] * real.astype(jnp.float32) + nonlocal_part).astype(jnp.bfloat16)
    section_three = jnp.dot(mixed, table_z, preferred_element_type=jnp.float32).astype(jnp.bfloat16)
    section_four = jnp.einsum(
        "by,oxyz->oxbz", table_y, section_three, preferred_element_type=jnp.float32
    ).astype(jnp.bfloat16)
    spectrum = jnp.einsum(
        "ax,oxyz->oayz",
        table_x,
        lax.all_to_all(section_four, "fft", split_axis=2, concat_axis=1, tiled=True),
        preferred_element_type=jnp.float32,
    )
    result = sphere_real[None] * (spectrum + kinetic[None] * masked.astype(jnp.float32))
    return result.astype(jnp.bfloat16)


def remote(source, target, send_sem, recv_sem, device, axis="fft"):
    return pltpu.make_async_remote_copy(
        src_ref=source,
        dst_ref=target,
        send_sem=send_sem,
        recv_sem=recv_sem,
        device_id={axis: device},
        device_id_type=MESH,
    )


def greet(device, axis="fft"):
    pl.semaphore_signal(
        pltpu.get_barrier_semaphore(), inc=1, device_id={axis: device}, device_id_type=MESH
    )


OWNERS = (0, 1, 6, 7)
HIGH = lax.Precision.HIGHEST


def matmul(left, right):
    return jnp.dot(left, right, preferred_element_type=jnp.float32)


def exact(left, right, dims=((1,), (0,))):
    return lax.dot_general(
        left, right, (dims, ((), ())), precision=HIGH, preferred_element_type=jnp.float32
    )


def swap(value):
    return jnp.transpose(value, (1, 0, 2))


def slab(at):
    return pl.ds(pl.multiple_of(at * 32, 32), 32)


def kernel(
    cell, count, dion, cell_row, atom_row, own_proj, table_in, table_out, coeff, sphere, potential,
    out,
    waves, ball, field, first, rows, cells, proj_parts, proj, spots, patches, high_part, low_part,
    planes_of, slot_atom, tables, fourth, back, gathered, ready, inside, kinetic,
    load_sem, out_sem, proj_send, proj_recv, first_send, first_recv, table_send, table_recv,
    back_send, back_recv, keep_sem,
):
    me, band = lax.axis_index("fft"), lax.axis_index("band")
    is_owner = (me < 2) | (me >= 6)
    own_block = jnp.where(me < 2, me, me - 4)

    def load_waves(orbital, half):
        return pltpu.make_async_copy(
            coeff.at[orbital, pl.ds(half * 192, 64)],
            waves.at[orbital, pl.ds(half * 64, 64)],
            load_sem.at[orbital, half],
        )

    def load_ball(half):
        return pltpu.make_async_copy(
            sphere.at[pl.ds(half * 192, 64)], ball.at[pl.ds(half * 64, 64)], load_sem.at[2, half]
        )

    load_field = pltpu.make_async_copy(potential, field, load_sem.at[3, 0])

    @pl.when(is_owner)
    def _():
        for half in range(2):
            load_ball(half).start()
            load_waves(0, half).start()
        for half in range(2):
            load_waves(1, half).start()

    for step in range(1, 8):
        greet((me + step) % 8)
    for step in range(1, 4):
        greet((band + step) % 4, "band")
    pl.semaphore_wait(pltpu.get_barrier_semaphore(), 10)

    def send_proj(step):
        return remote(
            own_proj,
            proj_parts.at[band],
            proj_send.at[step],
            proj_recv.at[step],
            (band + step) % 4,
            "band",
        )

    for step in range(1, 4):
        send_proj(step).start()

    def slot(orbital, at):
        return rows.at[orbital, :, slab(at)]

    def send_first(orbital, step):
        there = (me + step) % 8
        return remote(
            first.at[orbital, slab(there)],
            slot(orbital, own_block),
            first_send.at[orbital, step],
            first_recv.at[orbital, own_block],
            there,
        )

    def keep_first(orbital):
        return pltpu.make_async_copy(
            first.at[orbital, slab(me)], slot(orbital, own_block), keep_sem.at[0, orbital]
        )

    def section(orbital, carry):
        near = lax.broadcasted_iota(jnp.int32, (64, 32, 128), 2) < 64
        for half in range(2):
            load_waves(orbital, half).wait()
            part = pl.ds(half * 64, 64)
            value = waves[orbital, part].astype(jnp.float32) * ball[part].astype(jnp.float32)
            value = jnp.where(near, value[..., :128], value[..., 128:])
            spots[:, part, :] = swap(value).astype(jnp.bfloat16)

        def along_x(block, inner):
            part = pl.ds(pl.multiple_of(block * 64, 64), 64)
            table = table_in[part, :]
            for group in range(2):
                found = [matmul(table, spots[group * 16 + k]) for k in range(16)]
                value = swap(jnp.stack(found)).astype(jnp.bfloat16)
                first[orbital, part, group * 16 : group * 16 + 16, :] = value
            return inner

        lax.fori_loop(0, 4, along_x, 0)
        keep_first(orbital).start()

        @pl.when(orbital == 0)
        def _():
            for step in range(1, 8):
                send_first(orbital, step).start()

        return carry

    @pl.when(is_owner)
    def _():
        for half in range(2):
            load_ball(half).wait()
        lax.fori_loop(0, 2, section, 0)

    load_field.start()

    cells_at = cell_row[...]
    in_plane = (cells_at & 1) * 256 + ((cells_at & 511) >> 1)
    at_row = lax.broadcasted_iota(jnp.int32, (512, 512), 0)
    patches_at = (at_row == in_plane).astype(jnp.float32)
    tables_row = patches_at.astype(jnp.bfloat16)
    planes_row = jnp.broadcast_to((cells_at >> 9).astype(jnp.float32), (128, 512))
    planes_of[...] = jnp.transpose(planes_row, (1, 0))
    atoms = lax.broadcasted_iota(jnp.int32, (128, 512), 0)
    slots = lax.broadcasted_iota(jnp.int32, (128, 512), 1)
    chosen = ((atoms == atom_row[...]) & (slots < count[0])).astype(jnp.float32)
    slot_atom[...] = jnp.transpose(chosen, (1, 0))
    proj_parts[band] = own_proj[...]
    for step in range(1, 4):
        source = proj_parts.at[(band + 4 - step) % 4]
        copy = remote(
            own_proj, source, proj_send.at[step], proj_recv.at[step], (band + step) % 4, "band"
        )
        copy.wait_recv()
        copy.wait_send()
    lane_in = lax.broadcasted_iota(jnp.int32, (128, 128), 0)
    lane_out = lax.broadcasted_iota(jnp.int32, (128, 128), 1)
    for p in range(4):
        whole = jnp.zeros((512, 128), jnp.float32)
        for part in range(4):
            wanted = (lane_in == lane_out + 32 * (p - part)) & (lane_out // 32 == part)
            move = wanted.astype(jnp.float32).astype(jnp.bfloat16)
            whole = whole + matmul(proj_parts[part], move)
        proj[p] = whole
    load_field.wait()

    def squares(start, shape, axis):
        at = lax.broadcasted_iota(jnp.int32, shape, axis) + start
        return (frequency(at, 256).astype(jnp.float32) * (4.0 / 256)) ** 2

    def inner(value):
        near = lax.broadcasted_iota(jnp.int32, value.shape[:-1] + (128,), 2) < 64
        return jnp.where(near, value[..., :128], value[..., 128:])

    def kinetic_term(block, carry):
        lane = lax.broadcasted_iota(jnp.int32, (1, 1, 128), 2)
        lane_freq = jnp.where(lane < 64, lane, 128 - lane).astype(jnp.float32) * (4.0 / 256)
        energy = 2.0 * (
            squares(block * 32 + block // 2 * 128, (32, 1, 128), 0)
            + squares(me * 32, (1, 32, 128), 1)
            + lane_freq**2
        )
        near_ball = inner(ball[slab(block)].astype(jnp.float32))
        inside[slab(block)] = near_ball
        for orbital in range(2):
            masked = inner(waves[orbital, slab(block)].astype(jnp.float32)) * near_ball
            kinetic[orbital, slab(block)] = energy * masked
        return carry

    @pl.when(is_owner)
    def _():
        lax.fori_loop(0, 4, kinetic_term, 0)
        for step in range(1, 8):
            send_first(0, step).wait_send()
            send_first(1, step).start()

    def send_table(orbital, step):
        return remote(
            tables.at[orbital, me],
            tables.at[orbital, me],
            table_send.at[orbital, step],
            table_recv.at[orbital, step],
            (me + step) % 8,
        )

    def slots_back(orbital, device, part):
        return gathered.at[orbital, :, pl.ds(pl.multiple_of(device * 32 + part * 16, 16), 16)]

    def send_back(orbital, part, block, owner):
        return remote(
            back.at[orbital, part, block],
            slots_back(orbital, me, part),
            back_send.at[orbital, part, block],
            back_recv.at[orbital, part, me],
            owner,
        )

    def keep_back(orbital, part, block):
        return pltpu.make_async_copy(
            back.at[orbital, part, block],
            slots_back(orbital, me, part),
            keep_sem.at[1 + part, orbital],
        )

    def one_orbital(orbital, carry):
        for at, owner in enumerate(OWNERS):

            @pl.when(me != owner)
            def _(at=at, owner=owner):
                remote(
                    first.at[orbital, slab(0)],
                    slot(orbital, at),
                    first_send.at[orbital, 0],
                    first_recv.at[orbital, at],
                    owner,
                ).wait_recv()

        @pl.when(is_owner)
        def _():
            keep_first(orbital).wait()

        def to_plane(x, inner):
            second = matmul(table_in[...], rows[orbital, x]).astype(jnp.bfloat16)
            wide = matmul(second, table_out[...]).astype(jnp.bfloat16).astype(jnp.float32)
            base = pl.multiple_of(x * 512, 512)
            cells[pl.ds(base, 256), :] = wide[:, :128]
            cells[pl.ds(base + 256, 256), :] = wide[:, 128:]
            return inner

        lax.fori_loop(0, 32, to_plane, 0, unroll=4)

        def fetch(group, inner):
            base = pl.multiple_of(group * 8, 8)
            for k in range(8):
                at = cell[base + k]
                row = (at >> 9) * 512 + (at & 1) * 256 + ((at & 511) >> 1)
                patches[pl.ds(base + k, 1), :] = cells[pl.ds(row, 1), :]
            return inner

        lax.fori_loop(0, 64, fetch, 0)
        of_slot = slot_atom[...]
        ones = jnp.ones((8, 128), jnp.float32)
        for p in range(4):
            by_atom = exact(chosen, patches[...] * proj[p])
            tables[orbital, me, p : p + 1, :] = exact(ones, by_atom, ((1,), (1,)))[0:1]
        for step in range(1, 8):
            send_table(orbital, step).start()
        for step in range(1, 8):
            source = tables.at[orbital, (me + 8 - step) % 8]
            copy = remote(
                source,
                source,
                table_send.at[orbital, step],
                table_recv.at[orbital, step],
                (me + step) % 8,
            )
            copy.wait_recv()
            copy.wait_send()
        total = tables[orbital, 0]
        for other in range(1, 8):
            total = total + tables[orbital, other]
        strength = exact(of_slot, jnp.concatenate([total, total], axis=0), ((1,), (1,)))
        added = strength[:, 0:1] * dion[0] * proj[0]
        for p in range(1, 4):
            added = added + strength[:, p : p + 1] * dion[p] * proj[p]
        top = added.astype(jnp.bfloat16).astype(jnp.float32)
        high_part[...] = top
        low_part[...] = added - top

        def from_plane(x, inner):
            here = planes_of[...] == x.astype(jnp.float32)
            pieces = jnp.concatenate(
                [
                    jnp.where(here, high_part[...], 0.0).astype(jnp.bfloat16),
                    jnp.where(here, low_part[...], 0.0).astype(jnp.bfloat16),
                ],
                axis=1,
            )
            spread = matmul(tables_row, pieces)
            spread = spread[:, :128] + spread[:, 128:]
            base = pl.multiple_of(x * 512, 512)
            level = field[x]
            left = level[:, :128] * cells[pl.ds(base, 256), :] + spread[:256]
            right = level[:, 128:] * cells[pl.ds(base + 256, 256), :] + spread[256:]
            mixed = jnp.concatenate([left.astype(jnp.bfloat16), right.astype(jnp.bfloat16)], axis=1)
            third = matmul(mixed, table_in[...]).astype(jnp.bfloat16)
            fourth[x % 16] = matmul(table_out[...], third)
            return inner

        def half_slab(part, inner):
            lax.fori_loop(0, 16, lambda x, c: from_plane(part * 16 + x, c), 0, unroll=4)

            def turn(group, inmost):
                value = fourth[:, pl.ds(pl.multiple_of(group * 8, 8), 8), :]
                value = swap(value).astype(jnp.bfloat16)
                back[orbital, part, group // 4, pl.ds(group % 4 * 8, 8)] = value
                return inmost

            lax.fori_loop(0, 16, turn, 0, unroll=2)
            for block, owner in enumerate(OWNERS):

                @pl.when(me != owner)
                def _(block=block, owner=owner):
                    send_back(orbital, part, block, owner).start()

                @pl.when(me == owner)
                def _(block=block):
                    keep_back(orbital, part, block).start()

            return inner

        lax.fori_loop(0, 2, half_slab, 0)
        return carry

    lax.fori_loop(0, 2, one_orbital, 0)

    def write(step):
        return pltpu.make_async_copy(
            ready.at[step % 2], out.at[step // 4, slab(step % 4)], out_sem.at[step % 2]
        )

    def finish(step, carry):
        orbital, block = step // 4, step % 4

        @pl.when(block == 0)
        def _():
            for part in range(2):
                for other in range(1, 8):
                    sender = (me + other) % 8
                    remote(
                        back.at[orbital, part, 0],
                        slots_back(orbital, sender, part),
                        back_send.at[orbital, part, 0],
                        back_recv.at[orbital, part, sender],
                        sender,
                    ).wait_recv()
                keep_back(orbital, part, own_block).wait()

        @pl.when(step >= 2)
        def _():
            write(step - 2).wait()

        table = table_out[slab(block), :]
        for group in range(2):
            here = slice(group * 16, group * 16 + 16)
            found = [matmul(table, gathered[orbital, group * 16 + k]) for k in range(16)]
            spectrum = swap(jnp.stack(found))
            result = inside[slab(block), here] * spectrum + kinetic[orbital, slab(block), here]
            ready[step % 2, :, here] = result.astype(jnp.bfloat16)
        write(step).start()
        return carry

    @pl.when(is_owner)
    def _():
        lax.fori_loop(0, 8, finish, 0)
        write(6).wait()
        write(7).wait()
        for step in range(1, 8):
            send_first(1, step).wait_send()

    for orbital in range(2):
        for part in range(2):
            for block, owner in enumerate(OWNERS):

                @pl.when(me != owner)
                def _(orbital=orbital, part=part, block=block, owner=owner):
                    send_back(orbital, part, block, owner).wait_send()


def pad_kernel(owner, value, out):
    used = (owner[0] == 1) & (pl.program_id(1) % 3 == 0)

    @pl.when(used)
    def _():
        wide = value[0].astype(jnp.float32)
        near = lax.broadcasted_iota(jnp.int32, wide.shape, 2) < 64
        out[0, :, :, :128] = jnp.where(near, wide, 0.0).astype(jnp.bfloat16)
        out[0, :, :, 128:] = jnp.where(near, 0.0, wide).astype(jnp.bfloat16)

    @pl.when(jnp.logical_not(used))
    def _():
        out[...] = jnp.zeros_like(out)


def pad(owner, value, shape):
    return pl.pallas_call(
        pad_kernel,
        grid=(2, 4),
        out_shape=jax.ShapeDtypeStruct(shape, jnp.bfloat16),
        in_specs=[
            pl.BlockSpec(memory_space=pltpu.SMEM),
            pl.BlockSpec((1, 64, 32, 128), lambda o, b: (o, b // 2, 0, 0)),
        ],
        out_specs=pl.BlockSpec((1, 64, 32, 256), lambda o, b: (o, b, 0, 0)),
        compiler_params=pltpu.CompilerParams(vmem_limit_bytes=VMEM_BYTES),
        name="pad",
    )(owner, value)


def line_of_chips(coeff, sphere, potential, proj_values, tile_cell, tile_atom, tile_count, dion):
    table = cas_table(256)
    table_out = jnp.concatenate([table[:64], table[192:]], axis=0)
    smem = pl.BlockSpec(memory_space=pltpu.SMEM)
    vmem = pl.BlockSpec(memory_space=pltpu.VMEM)
    anywhere = pl.BlockSpec(memory_space=pl.ANY)
    dma = pltpu.SemaphoreType.DMA
    half, single = jnp.bfloat16, jnp.float32
    own_index = lax.axis_index("fft")
    is_owner = ((own_index < 2) | (own_index >= 6)).astype(jnp.int32)[None]
    result = pl.pallas_call(
        kernel,
        out_shape=jax.ShapeDtypeStruct((2, 128, 32, 128), half),
        in_specs=[smem] * 3 + [vmem] * 5 + [anywhere] * 3,
        out_specs=anywhere,
        scratch_shapes=[
            pltpu.VMEM((2, 128, 32, 256), half),
            pltpu.VMEM((128, 32, 256), jnp.int32),
            pltpu.VMEM((32, 256, 256), single),
            pltpu.VMEM((2, 256, 32, 128), half),
            pltpu.VMEM((2, 32, 128, 128), half),
            pltpu.VMEM((16384, 128), single),
            pltpu.VMEM((4, 512, 128), half),
            pltpu.VMEM((4, 512, 128), single),
            pltpu.VMEM((32, 128, 128), half),
            pltpu.VMEM((512, 128), single),
            pltpu.VMEM((512, 128), single),
            pltpu.VMEM((512, 128), single),
            pltpu.VMEM((512, 128), single),
            pltpu.VMEM((512, 128), single),
            pltpu.VMEM((2, 8, 4, 128), single),
            pltpu.VMEM((16, 128, 128), single),
            pltpu.VMEM((2, 2, 4, 32, 16, 128), half),
            pltpu.VMEM((2, 32, 256, 128), half),
            pltpu.VMEM((2, 32, 32, 128), half),
            pltpu.VMEM((128, 32, 128), single),
            pltpu.VMEM((2, 128, 32, 128), single),
            dma((4, 2)),
            dma((2,)),
            dma((4,)),
            dma((4,)),
            dma((2, 8)),
            dma((2, 4)),
            dma((2, 8)),
            dma((2, 8)),
            dma((2, 2, 4)),
            dma((2, 2, 8)),
            dma((3, 2)),
        ],
        compiler_params=pltpu.CompilerParams(
            collective_id=0, has_side_effects=True, vmem_limit_bytes=VMEM_BYTES
        ),
        name="hamiltonian",
    )(
        tile_cell,
        tile_count,
        dion,
        tile_cell[None, :],
        tile_atom[None, :],
        proj_values.reshape(512, 128),
        table_out.T,
        table_out,
        coeff,
        sphere,
        potential,
    )
    return pad(is_owner, result, coeff.shape)


def local(*values):
    coeff, slots, shards = values[0], values[4].shape[0], lax.axis_size("fft")
    if coeff.shape == (2, 256, 32, 256) and shards == 8 and slots == 512:
        return line_of_chips(*values)
    return general(*values)


def solution(mesh):
    in_specs = (
        P("band", None, "fft", None),
        P(None, "fft", None),
        P("fft", None, None),
        P("fft", None, "band"),
        P("fft"),
        P("fft"),
        P("fft"),
        P(),
    )
    out_specs = P("band", None, "fft", None)
    return jax.shard_map(local, mesh=mesh, in_specs=in_specs, out_specs=out_specs, check_vma=False)
```

```python
import math

import jax
import jax.numpy as jnp
from jax import lax
from jax.experimental import pallas as pl
from jax.experimental.pallas import tpu as pltpu
from jax.sharding import PartitionSpec as P

APD = 16
REACH = 3
MESH = pl.DeviceIdType.MESH
VMEM_BYTES = 58 * 2**20


def from_behind(value, axis, steps):
    count = lax.axis_size(axis)
    pairs = [(source, (source + steps) % count) for source in range(count)]
    return lax.ppermute(value, axis, pairs)


def cas_table(length):
    index = jnp.arange(length, dtype=jnp.int32)
    product = index[:, None] * index[None, :] % length
    angle = product.astype(jnp.float32) * (2.0 * math.pi / length)
    return ((jnp.cos(angle) + jnp.sin(angle)) * (1.0 / math.sqrt(length))).astype(jnp.bfloat16)


def frequency(index, length):
    return jnp.minimum(index, length - index)


def general(coeff, sphere, potential, proj_values, tile_cell, tile_atom, tile_count, dion):
    high = lax.Precision.HIGHEST
    orbitals, full_x, local_y, full_z = coeff.shape
    shards = lax.axis_size("fft")
    own_index = lax.axis_index("fft")
    full_y = local_y * shards
    table_x = cas_table(full_x)
    table_y = cas_table(full_y)
    table_z = cas_table(full_z)
    sphere_real = sphere.astype(jnp.float32)
    masked = (coeff.astype(jnp.float32) * sphere_real[None]).astype(jnp.bfloat16)
    row_x = frequency(jnp.arange(full_x, dtype=jnp.int32), full_x).astype(jnp.float32)
    row_y = frequency(own_index * local_y + jnp.arange(local_y, dtype=jnp.int32), full_y).astype(
        jnp.float32
    )
    row_z = frequency(jnp.arange(full_z, dtype=jnp.int32), full_z).astype(jnp.float32)
    kinetic = 2.0 * (
        (4.0 * row_x / full_x)[:, None, None] ** 2
        + (4.0 * row_y / full_y)[None, :, None] ** 2
        + (4.0 * row_z / full_z)[None, None, :] ** 2
    )
    section_one = jnp.einsum(
        "ax,oxyz->oayz", table_x, masked, preferred_element_type=jnp.float32
    ).astype(jnp.bfloat16)
    along_y = jnp.einsum(
        "by,oxyz->oxbz",
        table_y,
        lax.all_to_all(section_one, "fft", split_axis=1, concat_axis=2, tiled=True),
        preferred_element_type=jnp.float32,
    ).astype(jnp.bfloat16)
    real = jnp.dot(along_y, table_z, preferred_element_type=jnp.float32).astype(jnp.bfloat16)
    whole_proj = lax.all_gather(proj_values, "band", axis=2, tiled=True)
    flat = real.reshape(orbitals, -1, 128)
    patches = jnp.take(flat, tile_cell, axis=1)
    slots = tile_cell.shape[0]
    live = (jnp.arange(slots, dtype=jnp.int32) < tile_count[0]).astype(jnp.float32)
    partial_value = (
        jnp.einsum("otc,tpc->otp", patches, whole_proj, preferred_element_type=jnp.float32)
        * live[None, :, None]
    )
    width = (2 * REACH + 1) * APD
    home = tile_atom // APD
    local_atom = (home - own_index + REACH) % shards * APD + tile_atom % APD
    onehot = (local_atom[:, None] == jnp.arange(width, dtype=jnp.int32)[None, :]).astype(
        jnp.float32
    )
    table = jnp.einsum("otp,ta->oap", partial_value, onehot, precision=high)
    intersection = table
    for offset in range(-2 * REACH, 2 * REACH + 1):
        if offset != 0:
            arrived = from_behind(table, "fft", offset)
            first = max(0, -offset)
            last = min(2 * REACH, 2 * REACH - offset)
            intersection = intersection.at[:, first * APD : (last + 1) * APD].add(
                arrived[:, (first + offset) * APD : (last + offset + 1) * APD]
            )
    weights = intersection * dion[None, None, :]
    back = jnp.einsum("oap,ta->otp", weights, onehot, precision=high) * live[None, :, None]
    added = jnp.einsum("otp,tpc->otc", back, whole_proj.astype(jnp.float32), precision=high)
    nonlocal_part = (
        jnp.zeros(flat.shape, jnp.float32).at[:, tile_cell].add(added).reshape(real.shape)
    )
    mixed = (potential[None] * real.astype(jnp.float32) + nonlocal_part).astype(jnp.bfloat16)
    section_three = jnp.dot(mixed, table_z, preferred_element_type=jnp.float32).astype(jnp.bfloat16)
    section_four = jnp.einsum(
        "by,oxyz->oxbz", table_y, section_three, preferred_element_type=jnp.float32
    ).astype(jnp.bfloat16)
    spectrum = jnp.einsum(
        "ax,oxyz->oayz",
        table_x,
        lax.all_to_all(section_four, "fft", split_axis=2, concat_axis=1, tiled=True),
        preferred_element_type=jnp.float32,
    )
    result = sphere_real[None] * (spectrum + kinetic[None] * masked.astype(jnp.float32))
    return result.astype(jnp.bfloat16)


def remote(source, target, send_sem, recv_sem, device, axis="fft"):
    return pltpu.make_async_remote_copy(
        src_ref=source,
        dst_ref=target,
        send_sem=send_sem,
        recv_sem=recv_sem,
        device_id={axis: device},
        device_id_type=MESH,
    )


def greet(device, axis="fft"):
    pl.semaphore_signal(
        pltpu.get_barrier_semaphore(), inc=1, device_id={axis: device}, device_id_type=MESH
    )


OWNERS = (0, 1, 6, 7)
EARLY = 4
HIGH = lax.Precision.HIGHEST


def matmul(left, right):
    return jnp.dot(left, right, preferred_element_type=jnp.float32)


def exact(left, right, dims=((1,), (0,))):
    return lax.dot_general(
        left, right, (dims, ((), ())), precision=HIGH, preferred_element_type=jnp.float32
    )


def swap(value):
    return jnp.transpose(value, (1, 0, 2))


def slab(at):
    return pl.ds(pl.multiple_of(at * 32, 32), 32)


def kernel(
    cell, count, dion, cell_row, atom_row, own_proj, table_in, table_out, coeff, sphere, potential,
    out,
    waves, ball, field, first, rows, cells, proj_parts, proj, spots, patches, tiles,
    planes_of, slot_atom, tables, fourth, back, gathered, ready, inside, kinetic,
    load_sem, out_sem, proj_send, proj_recv, first_send, first_recv, table_send, table_recv,
    back_send, back_recv, keep_sem,
):
    me, band = lax.axis_index("fft"), lax.axis_index("band")
    is_owner = (me < 2) | (me >= 6)
    own_block = jnp.where(me < 2, me, me - 4)

    def load_waves(orbital, half):
        return pltpu.make_async_copy(
            coeff.at[orbital, pl.ds(half * 192, 64)],
            waves.at[orbital, pl.ds(half * 64, 64)],
            load_sem.at[orbital, half],
        )

    def load_ball(half):
        return pltpu.make_async_copy(
            sphere.at[pl.ds(half * 192, 64)], ball.at[pl.ds(half * 64, 64)], load_sem.at[2, half]
        )

    load_field = pltpu.make_async_copy(potential, field, load_sem.at[3, 0])

    @pl.when(is_owner)
    def _():
        for half in range(2):
            load_ball(half).start()
            load_waves(0, half).start()
        for half in range(2):
            load_waves(1, half).start()

    for step in range(1, 8):
        greet((me + step) % 8)
    for step in range(1, 4):
        greet((band + step) % 4, "band")
    pl.semaphore_wait(pltpu.get_barrier_semaphore(), 10)

    def send_proj(step):
        return remote(
            own_proj,
            proj_parts.at[band],
            proj_send.at[step],
            proj_recv.at[step],
            (band + step) % 4,
            "band",
        )

    for step in range(1, 4):
        send_proj(step).start()

    def slot(orbital, at):
        return rows.at[orbital, :, slab(at)]

    def send_first(orbital, step):
        there = (me + step) % 8
        return remote(
            first.at[orbital, slab(there)],
            slot(orbital, own_block),
            first_send.at[orbital, step],
            first_recv.at[orbital, own_block],
            there,
        )

    def keep_first(orbital):
        return pltpu.make_async_copy(
            first.at[orbital, slab(me)], slot(orbital, own_block), keep_sem.at[0, orbital]
        )

    def section(orbital, carry):
        near = lax.broadcasted_iota(jnp.int32, (64, 32, 128), 2) < 64
        for half in range(2):
            load_waves(orbital, half).wait()
            part = pl.ds(half * 64, 64)
            value = waves[orbital, part].astype(jnp.float32) * ball[part].astype(jnp.float32)
            value = jnp.where(near, value[..., :128], value[..., 128:])
            spots[:, part, :] = swap(value).astype(jnp.bfloat16)

        def along_x(block, inner):
            part = pl.ds(pl.multiple_of(block * 64, 64), 64)
            table = table_in[part, :]
            for group in range(2):
                found = [matmul(table, spots[group * 16 + k]) for k in range(16)]
                value = swap(jnp.stack(found)).astype(jnp.bfloat16)
                first[orbital, part, group * 16 : group * 16 + 16, :] = value
            return inner

        lax.fori_loop(0, 4, along_x, 0)
        keep_first(orbital).start()

        @pl.when(orbital == 0)
        def _():
            for step in range(1, 8):
                send_first(orbital, step).start()

        return carry

    @pl.when(is_owner)
    def _():
        for half in range(2):
            load_ball(half).wait()
        lax.fori_loop(0, 2, section, 0)

    load_field.start()

    cells_at = cell_row[...]
    in_plane = (cells_at & 1) * 256 + ((cells_at & 511) >> 1)
    at_row = lax.broadcasted_iota(jnp.int32, (512, 512), 0)
    patches_at = (at_row == in_plane).astype(jnp.float32)
    tables_row = patches_at.astype(jnp.bfloat16)
    planes_row = jnp.broadcast_to((cells_at >> 9).astype(jnp.float32), (128, 512))
    planes_of[...] = jnp.transpose(planes_row, (1, 0))
    atoms = lax.broadcasted_iota(jnp.int32, (128, 512), 0)
    slots = lax.broadcasted_iota(jnp.int32, (128, 512), 1)
    chosen = ((atoms == atom_row[...]) & (slots < count[0])).astype(jnp.float32)
    slot_atom[...] = jnp.transpose(chosen, (1, 0))
    proj_parts[band] = own_proj[...]
    for step in range(1, 4):
        source = proj_parts.at[(band + 4 - step) % 4]
        copy = remote(
            own_proj, source, proj_send.at[step], proj_recv.at[step], (band + step) % 4, "band"
        )
        copy.wait_recv()
        copy.wait_send()
    lane_in = lax.broadcasted_iota(jnp.int32, (128, 128), 0)
    lane_out = lax.broadcasted_iota(jnp.int32, (128, 128), 1)
    for p in range(4):
        whole = jnp.zeros((512, 128), jnp.float32)
        for part in range(4):
            wanted = (lane_in == lane_out + 32 * (p - part)) & (lane_out // 32 == part)
            move = wanted.astype(jnp.float32).astype(jnp.bfloat16)
            whole = whole + matmul(proj_parts[part], move)
        proj[p] = whole
    load_field.wait()

    def squares(start, shape, axis):
        at = lax.broadcasted_iota(jnp.int32, shape, axis) + start
        return (frequency(at, 256).astype(jnp.float32) * (4.0 / 256)) ** 2

    def inner(value):
        near = lax.broadcasted_iota(jnp.int32, value.shape[:-1] + (128,), 2) < 64
        return jnp.where(near, value[..., :128], value[..., 128:])

    def kinetic_term(block, carry):
        lane = lax.broadcasted_iota(jnp.int32, (1, 1, 128), 2)
        lane_freq = jnp.where(lane < 64, lane, 128 - lane).astype(jnp.float32) * (4.0 / 256)
        energy = 2.0 * (
            squares(block * 32 + block // 2 * 128, (32, 1, 128), 0)
            + squares(me * 32, (1, 32, 128), 1)
            + lane_freq**2
        )
        near_ball = inner(ball[slab(block)].astype(jnp.float32))
        inside[slab(block)] = near_ball
        for orbital in range(2):
            masked = inner(waves[orbital, slab(block)].astype(jnp.float32)) * near_ball
            kinetic[orbital, slab(block)] = energy * masked
        return carry

    @pl.when(is_owner)
    def _():
        lax.fori_loop(0, 4, kinetic_term, 0)
        for step in range(1, 8):
            send_first(0, step).wait_send()
        for step in range(1, EARLY):
            send_first(1, step).start()

    def send_table(orbital, step):
        return remote(
            tables.at[orbital, me],
            tables.at[orbital, me],
            table_send.at[orbital, step],
            table_recv.at[orbital, step],
            (me + step) % 8,
        )

    def slots_back(orbital, device, part):
        return gathered.at[orbital, :, pl.ds(pl.multiple_of(device * 32 + part * 16, 16), 16)]

    def send_back(orbital, part, block, owner):
        return remote(
            back.at[orbital, part, block],
            slots_back(orbital, me, part),
            back_send.at[orbital, part, block],
            back_recv.at[orbital, part, me],
            owner,
        )

    def keep_back(orbital, part, block):
        return pltpu.make_async_copy(
            back.at[orbital, part, block],
            slots_back(orbital, me, part),
            keep_sem.at[1 + part, orbital],
        )

    def one_orbital(orbital, carry):
        for at, owner in enumerate(OWNERS):

            @pl.when(me != owner)
            def _(at=at, owner=owner):
                remote(
                    first.at[orbital, slab(0)],
                    slot(orbital, at),
                    first_send.at[orbital, 0],
                    first_recv.at[orbital, at],
                    owner,
                ).wait_recv()

        @pl.when(is_owner)
        def _():
            keep_first(orbital).wait()

        def to_plane(x, inner):
            second = matmul(table_in[...], rows[orbital, x]).astype(jnp.bfloat16)
            wide = matmul(second, table_out[...]).astype(jnp.bfloat16).astype(jnp.float32)
            base = pl.multiple_of(x * 512, 512)
            cells[pl.ds(base, 256), :] = wide[:, :128]
            cells[pl.ds(base + 256, 256), :] = wide[:, 128:]
            return inner

        lax.fori_loop(0, 32, to_plane, 0, unroll=4)

        def fetch(group, inner):
            base = pl.multiple_of(group * 8, 8)
            for k in range(8):
                at = cell[base + k]
                row = (at >> 9) * 512 + (at & 1) * 256 + ((at & 511) >> 1)
                patches[pl.ds(base + k, 1), :] = cells[pl.ds(row, 1), :]
            return inner

        lax.fori_loop(0, 64, fetch, 0)
        of_slot = slot_atom[...]
        ones = jnp.ones((8, 128), jnp.float32)
        for p in range(4):
            by_atom = exact(chosen, patches[...] * proj[p])
            tables[orbital, me, p : p + 1, :] = exact(ones, by_atom, ((1,), (1,)))[0:1]
        for step in range(1, 8):
            send_table(orbital, step).start()

        @pl.when(is_owner & (orbital == 0))
        def _():
            for step in range(EARLY, 8):
                send_first(1, step).start()

        for step in range(1, 8):
            source = tables.at[orbital, (me + 8 - step) % 8]
            copy = remote(
                source,
                source,
                table_send.at[orbital, step],
                table_recv.at[orbital, step],
                (me + step) % 8,
            )
            copy.wait_recv()
            copy.wait_send()
        total = tables[orbital, 0]
        for other in range(1, 8):
            total = total + tables[orbital, other]
        strength = exact(of_slot, jnp.concatenate([total, total], axis=0), ((1,), (1,)))
        added = strength[:, 0:1] * dion[0] * proj[0]
        for p in range(1, 4):
            added = added + strength[:, p : p + 1] * dion[p] * proj[p]
        tiles[...] = added

        def from_planes(pair, inner):
            pieces = [
                jnp.where(planes_of[...] == (2 * pair + k).astype(jnp.float32), tiles[...], 0.0)
                for k in range(2)
            ]
            pieces = jnp.concatenate([piece.astype(jnp.bfloat16) for piece in pieces], axis=1)
            both = matmul(tables_row, pieces)
            for k in range(2):
                from_plane(2 * pair + k, both[:, k * 128 : k * 128 + 128])
            return inner

        def from_plane(x, spread):
            base = pl.multiple_of(x * 512, 512)
            level = field[x]
            left = level[:, :128] * cells[pl.ds(base, 256), :] + spread[:256]
            right = level[:, 128:] * cells[pl.ds(base + 256, 256), :] + spread[256:]
            mixed = jnp.concatenate([left.astype(jnp.bfloat16), right.astype(jnp.bfloat16)], axis=1)
            third = matmul(mixed, table_in[...]).astype(jnp.bfloat16)
            fourth[x % 16] = matmul(table_out[...], third)

        def half_slab(part, inner):
            lax.fori_loop(0, 8, lambda x, c: from_planes(part * 8 + x, c), 0, unroll=2)

            def turn(group, inmost):
                value = fourth[:, pl.ds(pl.multiple_of(group * 8, 8), 8), :]
                value = swap(value).astype(jnp.bfloat16)
                back[orbital, part, group // 4, pl.ds(group % 4 * 8, 8)] = value
                return inmost

            lax.fori_loop(0, 16, turn, 0, unroll=2)
            for block, owner in enumerate(OWNERS):

                @pl.when(me != owner)
                def _(block=block, owner=owner):
                    send_back(orbital, part, block, owner).start()

                @pl.when(me == owner)
                def _(block=block):
                    keep_back(orbital, part, block).start()

            return inner

        lax.fori_loop(0, 2, half_slab, 0)
        return carry

    lax.fori_loop(0, 2, one_orbital, 0)

    def write(step):
        return pltpu.make_async_copy(
            ready.at[step % 2], out.at[step // 4, slab(step % 4)], out_sem.at[step % 2]
        )

    def finish(step, carry):
        orbital, block = step // 4, step % 4

        @pl.when(block == 0)
        def _():
            for part in range(2):
                for other in range(1, 8):
                    sender = (me + other) % 8
                    remote(
                        back.at[orbital, part, 0],
                        slots_back(orbital, sender, part),
                        back_send.at[orbital, part, 0],
                        back_recv.at[orbital, part, sender],
                        sender,
                    ).wait_recv()
                keep_back(orbital, part, own_block).wait()

        @pl.when(step >= 2)
        def _():
            write(step - 2).wait()

        table = table_out[slab(block), :]
        for group in range(2):
            here = slice(group * 16, group * 16 + 16)
            found = [matmul(table, gathered[orbital, group * 16 + k]) for k in range(16)]
            spectrum = swap(jnp.stack(found))
            result = inside[slab(block), here] * spectrum + kinetic[orbital, slab(block), here]
            ready[step % 2, :, here] = result.astype(jnp.bfloat16)
        write(step).start()
        return carry

    @pl.when(is_owner)
    def _():
        lax.fori_loop(0, 8, finish, 0)
        write(6).wait()
        write(7).wait()
        for step in range(1, 8):
            send_first(1, step).wait_send()

    for orbital in range(2):
        for part in range(2):
            for block, owner in enumerate(OWNERS):

                @pl.when(me != owner)
                def _(orbital=orbital, part=part, block=block, owner=owner):
                    send_back(orbital, part, block, owner).wait_send()


def pad_kernel(owner, value, out):
    used = (owner[0] == 1) & (pl.program_id(1) % 3 == 0)

    @pl.when(used)
    def _():
        wide = value[0].astype(jnp.float32)
        near = lax.broadcasted_iota(jnp.int32, wide.shape, 2) < 64
        out[0, :, :, :128] = jnp.where(near, wide, 0.0).astype(jnp.bfloat16)
        out[0, :, :, 128:] = jnp.where(near, 0.0, wide).astype(jnp.bfloat16)

    @pl.when(jnp.logical_not(used))
    def _():
        out[...] = jnp.zeros_like(out)


def pad(owner, value, shape):
    return pl.pallas_call(
        pad_kernel,
        grid=(2, 4),
        out_shape=jax.ShapeDtypeStruct(shape, jnp.bfloat16),
        in_specs=[
            pl.BlockSpec(memory_space=pltpu.SMEM),
            pl.BlockSpec((1, 64, 32, 128), lambda o, b: (o, b // 2, 0, 0)),
        ],
        out_specs=pl.BlockSpec((1, 64, 32, 256), lambda o, b: (o, b, 0, 0)),
        compiler_params=pltpu.CompilerParams(vmem_limit_bytes=VMEM_BYTES),
        name="pad",
    )(owner, value)


def line_of_chips(coeff, sphere, potential, proj_values, tile_cell, tile_atom, tile_count, dion):
    table = cas_table(256)
    table_out = jnp.concatenate([table[:64], table[192:]], axis=0)
    smem = pl.BlockSpec(memory_space=pltpu.SMEM)
    vmem = pl.BlockSpec(memory_space=pltpu.VMEM)
    anywhere = pl.BlockSpec(memory_space=pl.ANY)
    dma = pltpu.SemaphoreType.DMA
    half, single = jnp.bfloat16, jnp.float32
    own_index = lax.axis_index("fft")
    is_owner = ((own_index < 2) | (own_index >= 6)).astype(jnp.int32)[None]
    result = pl.pallas_call(
        kernel,
        out_shape=jax.ShapeDtypeStruct((2, 128, 32, 128), half),
        in_specs=[smem] * 3 + [vmem] * 5 + [anywhere] * 3,
        out_specs=anywhere,
        scratch_shapes=[
            pltpu.VMEM((2, 128, 32, 256), half),
            pltpu.VMEM((128, 32, 256), jnp.int32),
            pltpu.VMEM((32, 256, 256), single),
            pltpu.VMEM((2, 256, 32, 128), half),
            pltpu.VMEM((2, 32, 128, 128), half),
            pltpu.VMEM((16384, 128), single),
            pltpu.VMEM((4, 512, 128), half),
            pltpu.VMEM((4, 512, 128), single),
            pltpu.VMEM((32, 128, 128), half),
            pltpu.VMEM((512, 128), single),
            pltpu.VMEM((512, 128), single),
            pltpu.VMEM((512, 128), single),
            pltpu.VMEM((512, 128), single),
            pltpu.VMEM((2, 8, 4, 128), single),
            pltpu.VMEM((16, 128, 128), single),
            pltpu.VMEM((2, 2, 4, 32, 16, 128), half),
            pltpu.VMEM((2, 32, 256, 128), half),
            pltpu.VMEM((2, 32, 32, 128), half),
            pltpu.VMEM((128, 32, 128), single),
            pltpu.VMEM((2, 128, 32, 128), single),
            dma((4, 2)),
            dma((2,)),
            dma((4,)),
            dma((4,)),
            dma((2, 8)),
            dma((2, 4)),
            dma((2, 8)),
            dma((2, 8)),
            dma((2, 2, 4)),
            dma((2, 2, 8)),
            dma((3, 2)),
        ],
        compiler_params=pltpu.CompilerParams(
            collective_id=0, has_side_effects=True, vmem_limit_bytes=VMEM_BYTES
        ),
        name="hamiltonian",
    )(
        tile_cell,
        tile_count,
        dion,
        tile_cell[None, :],
        tile_atom[None, :],
        proj_values.reshape(512, 128),
        table_out.T,
        table_out,
        coeff,
        sphere,
        potential,
    )
    return pad(is_owner, result, coeff.shape)


def local(*values):
    coeff, slots, shards = values[0], values[4].shape[0], lax.axis_size("fft")
    if coeff.shape == (2, 256, 32, 256) and shards == 8 and slots == 512:
        return line_of_chips(*values)
    return general(*values)


def solution(mesh):
    in_specs = (
        P("band", None, "fft", None),
        P(None, "fft", None),
        P("fft", None, None),
        P("fft", None, "band"),
        P("fft"),
        P("fft"),
        P("fft"),
        P(),
    )
    out_specs = P("band", None, "fft", None)
    return jax.shard_map(local, mesh=mesh, in_specs=in_specs, out_specs=out_specs, check_vma=False)
```

```python
import math

import jax
import jax.numpy as jnp
from jax import lax
from jax.experimental import pallas as pl
from jax.experimental.pallas import tpu as pltpu
from jax.sharding import PartitionSpec as P

APD = 16
REACH = 3
MESH = pl.DeviceIdType.MESH
VMEM_BYTES = 58 * 2**20


def from_behind(value, axis, steps):
    count = lax.axis_size(axis)
    pairs = [(source, (source + steps) % count) for source in range(count)]
    return lax.ppermute(value, axis, pairs)


def cas_table(length):
    index = jnp.arange(length, dtype=jnp.int32)
    product = index[:, None] * index[None, :] % length
    angle = product.astype(jnp.float32) * (2.0 * math.pi / length)
    return ((jnp.cos(angle) + jnp.sin(angle)) * (1.0 / math.sqrt(length))).astype(jnp.bfloat16)


def frequency(index, length):
    return jnp.minimum(index, length - index)


def general(coeff, sphere, potential, proj_values, tile_cell, tile_atom, tile_count, dion):
    high = lax.Precision.HIGHEST
    orbitals, full_x, local_y, full_z = coeff.shape
    shards = lax.axis_size("fft")
    own_index = lax.axis_index("fft")
    full_y = local_y * shards
    table_x = cas_table(full_x)
    table_y = cas_table(full_y)
    table_z = cas_table(full_z)
    sphere_real = sphere.astype(jnp.float32)
    masked = (coeff.astype(jnp.float32) * sphere_real[None]).astype(jnp.bfloat16)
    row_x = frequency(jnp.arange(full_x, dtype=jnp.int32), full_x).astype(jnp.float32)
    row_y = frequency(own_index * local_y + jnp.arange(local_y, dtype=jnp.int32), full_y).astype(
        jnp.float32
    )
    row_z = frequency(jnp.arange(full_z, dtype=jnp.int32), full_z).astype(jnp.float32)
    kinetic = 2.0 * (
        (4.0 * row_x / full_x)[:, None, None] ** 2
        + (4.0 * row_y / full_y)[None, :, None] ** 2
        + (4.0 * row_z / full_z)[None, None, :] ** 2
    )
    section_one = jnp.einsum(
        "ax,oxyz->oayz", table_x, masked, preferred_element_type=jnp.float32
    ).astype(jnp.bfloat16)
    along_y = jnp.einsum(
        "by,oxyz->oxbz",
        table_y,
        lax.all_to_all(section_one, "fft", split_axis=1, concat_axis=2, tiled=True),
        preferred_element_type=jnp.float32,
    ).astype(jnp.bfloat16)
    real = jnp.dot(along_y, table_z, preferred_element_type=jnp.float32).astype(jnp.bfloat16)
    whole_proj = lax.all_gather(proj_values, "band", axis=2, tiled=True)
    flat = real.reshape(orbitals, -1, 128)
    patches = jnp.take(flat, tile_cell, axis=1)
    slots = tile_cell.shape[0]
    live = (jnp.arange(slots, dtype=jnp.int32) < tile_count[0]).astype(jnp.float32)
    partial_value = (
        jnp.einsum("otc,tpc->otp", patches, whole_proj, preferred_element_type=jnp.float32)
        * live[None, :, None]
    )
    width = (2 * REACH + 1) * APD
    home = tile_atom // APD
    local_atom = (home - own_index + REACH) % shards * APD + tile_atom % APD
    onehot = (local_atom[:, None] == jnp.arange(width, dtype=jnp.int32)[None, :]).astype(
        jnp.float32
    )
    table = jnp.einsum("otp,ta->oap", partial_value, onehot, precision=high)
    intersection = table
    for offset in range(-2 * REACH, 2 * REACH + 1):
        if offset != 0:
            arrived = from_behind(table, "fft", offset)
            first = max(0, -offset)
            last = min(2 * REACH, 2 * REACH - offset)
            intersection = intersection.at[:, first * APD : (last + 1) * APD].add(
                arrived[:, (first + offset) * APD : (last + offset + 1) * APD]
            )
    weights = intersection * dion[None, None, :]
    back = jnp.einsum("oap,ta->otp", weights, onehot, precision=high) * live[None, :, None]
    added = jnp.einsum("otp,tpc->otc", back, whole_proj.astype(jnp.float32), precision=high)
    nonlocal_part = (
        jnp.zeros(flat.shape, jnp.float32).at[:, tile_cell].add(added).reshape(real.shape)
    )
    mixed = (potential[None] * real.astype(jnp.float32) + nonlocal_part).astype(jnp.bfloat16)
    section_three = jnp.dot(mixed, table_z, preferred_element_type=jnp.float32).astype(jnp.bfloat16)
    section_four = jnp.einsum(
        "by,oxyz->oxbz", table_y, section_three, preferred_element_type=jnp.float32
    ).astype(jnp.bfloat16)
    spectrum = jnp.einsum(
        "ax,oxyz->oayz",
        table_x,
        lax.all_to_all(section_four, "fft", split_axis=2, concat_axis=1, tiled=True),
        preferred_element_type=jnp.float32,
    )
    result = sphere_real[None] * (spectrum + kinetic[None] * masked.astype(jnp.float32))
    return result.astype(jnp.bfloat16)


def remote(source, target, send_sem, recv_sem, device, axis="fft"):
    return pltpu.make_async_remote_copy(
        src_ref=source,
        dst_ref=target,
        send_sem=send_sem,
        recv_sem=recv_sem,
        device_id={axis: device},
        device_id_type=MESH,
    )


def greet(device, axis="fft"):
    pl.semaphore_signal(
        pltpu.get_barrier_semaphore(), inc=1, device_id={axis: device}, device_id_type=MESH
    )


OWNERS = (0, 1, 6, 7)
EARLY = 4
HIGH = lax.Precision.HIGHEST


def matmul(left, right):
    return jnp.dot(left, right, preferred_element_type=jnp.float32)


def exact(left, right, dims=((1,), (0,))):
    return lax.dot_general(
        left, right, (dims, ((), ())), precision=HIGH, preferred_element_type=jnp.float32
    )


def swap(value):
    return jnp.transpose(value, (1, 0, 2))


def slab(at):
    return pl.ds(pl.multiple_of(at * 32, 32), 32)


def kernel(
    cell, count, dion, cell_row, atom_row, own_proj, table_in, table_out, coeff, sphere, potential,
    out,
    waves, ball, field, first, rows, cells, proj_parts, proj, spots, patches, tiles,
    planes_of, slot_atom, tables, fourth, back, gathered, ready, inside, kinetic,
    load_sem, out_sem, proj_send, proj_recv, first_send, first_recv, table_send, table_recv,
    back_send, back_recv, keep_sem,
):
    me, band = lax.axis_index("fft"), lax.axis_index("band")
    is_owner = (me < 2) | (me >= 6)
    own_block = jnp.where(me < 2, me, me - 4)

    def load_waves(orbital, half):
        return pltpu.make_async_copy(
            coeff.at[orbital, pl.ds(half * 192, 64)],
            waves.at[orbital, pl.ds(half * 64, 64)],
            load_sem.at[orbital, half],
        )

    def load_ball(half):
        return pltpu.make_async_copy(
            sphere.at[pl.ds(half * 192, 64)], ball.at[pl.ds(half * 64, 64)], load_sem.at[2, half]
        )

    load_field = pltpu.make_async_copy(potential, field, load_sem.at[3, 0])

    @pl.when(is_owner)
    def _():
        for half in range(2):
            load_ball(half).start()
            load_waves(0, half).start()
        for half in range(2):
            load_waves(1, half).start()

    for step in range(1, 8):
        greet((me + step) % 8)
    for step in range(1, 4):
        greet((band + step) % 4, "band")
    pl.semaphore_wait(pltpu.get_barrier_semaphore(), 10)

    def send_proj(step):
        return remote(
            own_proj,
            proj_parts.at[band],
            proj_send.at[step],
            proj_recv.at[step],
            (band + step) % 4,
            "band",
        )

    for step in range(1, 4):
        send_proj(step).start()

    def slot(orbital, at):
        return rows.at[orbital, :, slab(at)]

    def send_first(orbital, step):
        there = (me + step) % 8
        return remote(
            first.at[orbital, slab(there)],
            slot(orbital, own_block),
            first_send.at[orbital, step],
            first_recv.at[orbital, own_block],
            there,
        )

    def keep_first(orbital):
        return pltpu.make_async_copy(
            first.at[orbital, slab(me)], slot(orbital, own_block), keep_sem.at[0, orbital]
        )

    def section(orbital, carry):
        near = lax.broadcasted_iota(jnp.int32, (64, 32, 128), 2) < 64
        for half in range(2):
            load_waves(orbital, half).wait()
            part = pl.ds(half * 64, 64)
            value = waves[orbital, part].astype(jnp.float32) * ball[part].astype(jnp.float32)
            value = jnp.where(near, value[..., :128], value[..., 128:])
            spots[:, part, :] = swap(value).astype(jnp.bfloat16)

        def along_x(block, inner):
            part = pl.ds(pl.multiple_of(block * 64, 64), 64)
            table = table_in[part, :]
            for group in range(2):
                found = [matmul(table, spots[group * 16 + k]) for k in range(16)]
                value = swap(jnp.stack(found)).astype(jnp.bfloat16)
                first[orbital, part, group * 16 : group * 16 + 16, :] = value
            for k in range(2):
                step = (2 * block + k + 8 - me) % 8

                @pl.when((orbital == 0) & (step > 0))
                def _(step=step):
                    send_first(0, step).start()

            return inner

        lax.fori_loop(0, 4, along_x, 0)
        keep_first(orbital).start()
        return carry

    @pl.when(is_owner)
    def _():
        for half in range(2):
            load_ball(half).wait()
        lax.fori_loop(0, 2, section, 0)

    load_field.start()

    cells_at = cell_row[...]
    in_plane = (cells_at & 1) * 256 + ((cells_at & 511) >> 1)
    at_row = lax.broadcasted_iota(jnp.int32, (512, 512), 0)
    patches_at = (at_row == in_plane).astype(jnp.float32)
    tables_row = patches_at.astype(jnp.bfloat16)
    planes_row = jnp.broadcast_to((cells_at >> 9).astype(jnp.float32), (128, 512))
    planes_of[...] = jnp.transpose(planes_row, (1, 0))
    atoms = lax.broadcasted_iota(jnp.int32, (128, 512), 0)
    slots = lax.broadcasted_iota(jnp.int32, (128, 512), 1)
    chosen = ((atoms == atom_row[...]) & (slots < count[0])).astype(jnp.float32)
    slot_atom[...] = jnp.transpose(chosen, (1, 0))
    proj_parts[band] = own_proj[...]
    for step in range(1, 4):
        source = proj_parts.at[(band + 4 - step) % 4]
        copy = remote(
            own_proj, source, proj_send.at[step], proj_recv.at[step], (band + step) % 4, "band"
        )
        copy.wait_recv()
        copy.wait_send()
    lane_in = lax.broadcasted_iota(jnp.int32, (128, 128), 0)
    lane_out = lax.broadcasted_iota(jnp.int32, (128, 128), 1)
    for p in range(4):
        whole = jnp.zeros((512, 128), jnp.float32)
        for part in range(4):
            wanted = (lane_in == lane_out + 32 * (p - part)) & (lane_out // 32 == part)
            move = wanted.astype(jnp.float32).astype(jnp.bfloat16)
            whole = whole + matmul(proj_parts[part], move)
        proj[p] = whole
    load_field.wait()

    def squares(start, shape, axis):
        at = lax.broadcasted_iota(jnp.int32, shape, axis) + start
        return (frequency(at, 256).astype(jnp.float32) * (4.0 / 256)) ** 2

    def inner(value):
        near = lax.broadcasted_iota(jnp.int32, value.shape[:-1] + (128,), 2) < 64
        return jnp.where(near, value[..., :128], value[..., 128:])

    def kinetic_term(block, carry):
        lane = lax.broadcasted_iota(jnp.int32, (1, 1, 128), 2)
        lane_freq = jnp.where(lane < 64, lane, 128 - lane).astype(jnp.float32) * (4.0 / 256)
        energy = 2.0 * (
            squares(block * 32 + block // 2 * 128, (32, 1, 128), 0)
            + squares(me * 32, (1, 32, 128), 1)
            + lane_freq**2
        )
        near_ball = inner(ball[slab(block)].astype(jnp.float32))
        inside[slab(block)] = near_ball
        for orbital in range(2):
            masked = inner(waves[orbital, slab(block)].astype(jnp.float32)) * near_ball
            kinetic[orbital, slab(block)] = energy * masked
        return carry

    @pl.when(is_owner)
    def _():
        lax.fori_loop(0, 4, kinetic_term, 0)
        for step in range(1, 8):
            send_first(0, step).wait_send()
        for step in range(1, EARLY):
            send_first(1, step).start()

    def send_table(orbital, step):
        return remote(
            tables.at[orbital, me],
            tables.at[orbital, me],
            table_send.at[orbital, step],
            table_recv.at[orbital, step],
            (me + step) % 8,
        )

    def slots_back(orbital, device, part):
        return gathered.at[orbital, :, pl.ds(pl.multiple_of(device * 32 + part * 16, 16), 16)]

    def send_back(orbital, part, block, owner):
        return remote(
            back.at[orbital, part, block],
            slots_back(orbital, me, part),
            back_send.at[orbital, part, block],
            back_recv.at[orbital, part, me],
            owner,
        )

    def keep_back(orbital, part, block):
        return pltpu.make_async_copy(
            back.at[orbital, part, block],
            slots_back(orbital, me, part),
            keep_sem.at[1 + part, orbital],
        )

    def one_orbital(orbital, carry):
        for at, owner in enumerate(OWNERS):

            @pl.when(me != owner)
            def _(at=at, owner=owner):
                remote(
                    first.at[orbital, slab(0)],
                    slot(orbital, at),
                    first_send.at[orbital, 0],
                    first_recv.at[orbital, at],
                    owner,
                ).wait_recv()

        @pl.when(is_owner)
        def _():
            keep_first(orbital).wait()

        def to_plane(x, inner):
            second = matmul(table_in[...], rows[orbital, x]).astype(jnp.bfloat16)
            wide = matmul(second, table_out[...]).astype(jnp.bfloat16).astype(jnp.float32)
            base = pl.multiple_of(x * 512, 512)
            cells[pl.ds(base, 256), :] = wide[:, :128]
            cells[pl.ds(base + 256, 256), :] = wide[:, 128:]
            return inner

        lax.fori_loop(0, 32, to_plane, 0, unroll=4)

        def fetch(group, inner):
            base = pl.multiple_of(group * 8, 8)
            for k in range(8):
                at = cell[base + k]
                row = (at >> 9) * 512 + (at & 1) * 256 + ((at & 511) >> 1)
                patches[pl.ds(base + k, 1), :] = cells[pl.ds(row, 1), :]
            return inner

        lax.fori_loop(0, 64, fetch, 0)
        of_slot = slot_atom[...]
        ones = jnp.ones((8, 128), jnp.float32)
        for p in range(4):
            by_atom = exact(chosen, patches[...] * proj[p])
            tables[orbital, me, p : p + 1, :] = exact(ones, by_atom, ((1,), (1,)))[0:1]
        for step in range(1, 8):
            send_table(orbital, step).start()

        @pl.when(is_owner & (orbital == 0))
        def _():
            for step in range(EARLY, 8):
                send_first(1, step).start()

        for block in (1, 3):

            @pl.when((orbital == 1) & (me != OWNERS[block]))
            def _(block=block):
                send_back(0, 1, block, OWNERS[block]).start()

        for step in range(1, 8):
            source = tables.at[orbital, (me + 8 - step) % 8]
            copy = remote(
                source,
                source,
                table_send.at[orbital, step],
                table_recv.at[orbital, step],
                (me + step) % 8,
            )
            copy.wait_recv()
            copy.wait_send()
        total = tables[orbital, 0]
        for other in range(1, 8):
            total = total + tables[orbital, other]
        strength = exact(of_slot, jnp.concatenate([total, total], axis=0), ((1,), (1,)))
        added = strength[:, 0:1] * dion[0] * proj[0]
        for p in range(1, 4):
            added = added + strength[:, p : p + 1] * dion[p] * proj[p]
        tiles[...] = added

        def from_planes(pair, inner):
            pieces = [
                jnp.where(planes_of[...] == (2 * pair + k).astype(jnp.float32), tiles[...], 0.0)
                for k in range(2)
            ]
            pieces = jnp.concatenate([piece.astype(jnp.bfloat16) for piece in pieces], axis=1)
            both = matmul(tables_row, pieces)
            for k in range(2):
                from_plane(2 * pair + k, both[:, k * 128 : k * 128 + 128])
            return inner

        def from_plane(x, spread):
            base = pl.multiple_of(x * 512, 512)
            level = field[x]
            left = level[:, :128] * cells[pl.ds(base, 256), :] + spread[:256]
            right = level[:, 128:] * cells[pl.ds(base + 256, 256), :] + spread[256:]
            mixed = jnp.concatenate([left.astype(jnp.bfloat16), right.astype(jnp.bfloat16)], axis=1)
            third = matmul(mixed, table_in[...]).astype(jnp.bfloat16)
            fourth[x % 16] = matmul(table_out[...], third)

        def half_slab(part, inner):
            lax.fori_loop(0, 8, lambda x, c: from_planes(part * 8 + x, c), 0, unroll=2)

            def turn(group, inmost):
                value = fourth[:, pl.ds(pl.multiple_of(group * 8, 8), 8), :]
                value = swap(value).astype(jnp.bfloat16)
                back[orbital, part, group // 4, pl.ds(group % 4 * 8, 8)] = value
                return inmost

            lax.fori_loop(0, 16, turn, 0, unroll=2)
            for block, owner in enumerate(OWNERS):

                later = (orbital == 0) & (part == 1) & (block % 2 == 1)

                @pl.when((me != owner) & jnp.logical_not(later))
                def _(block=block, owner=owner):
                    send_back(orbital, part, block, owner).start()

                @pl.when(me == owner)
                def _(block=block):
                    keep_back(orbital, part, block).start()

            return inner

        lax.fori_loop(0, 2, half_slab, 0)
        return carry

    lax.fori_loop(0, 2, one_orbital, 0)

    def write(step):
        return pltpu.make_async_copy(
            ready.at[step % 2], out.at[step // 4, slab(step % 4)], out_sem.at[step % 2]
        )

    def finish(step, carry):
        orbital, block = step // 4, step % 4

        @pl.when(block == 0)
        def _():
            for part in range(2):
                for other in range(1, 8):
                    sender = (me + other) % 8
                    remote(
                        back.at[orbital, part, 0],
                        slots_back(orbital, sender, part),
                        back_send.at[orbital, part, 0],
                        back_recv.at[orbital, part, sender],
                        sender,
                    ).wait_recv()
                keep_back(orbital, part, own_block).wait()

        @pl.when(step >= 2)
        def _():
            write(step - 2).wait()

        table = table_out[slab(block), :]
        for group in range(2):
            here = slice(group * 16, group * 16 + 16)
            found = [matmul(table, gathered[orbital, group * 16 + k]) for k in range(16)]
            spectrum = swap(jnp.stack(found))
            result = inside[slab(block), here] * spectrum + kinetic[orbital, slab(block), here]
            ready[step % 2, :, here] = result.astype(jnp.bfloat16)
        write(step).start()
        return carry

    @pl.when(is_owner)
    def _():
        lax.fori_loop(0, 8, finish, 0)
        write(6).wait()
        write(7).wait()
        for step in range(1, 8):
            send_first(1, step).wait_send()

    for orbital in range(2):
        for part in range(2):
            for block, owner in enumerate(OWNERS):

                @pl.when(me != owner)
                def _(orbital=orbital, part=part, block=block, owner=owner):
                    send_back(orbital, part, block, owner).wait_send()


def pad_kernel(value, out, empty, wide, sems):
    me = lax.axis_index("fft")
    is_owner = (me < 2) | (me >= 6)
    empty[...] = jnp.zeros_like(empty)

    def clear(orbital, part):
        return pltpu.make_async_copy(
            empty, out.at[orbital, pl.ds(part * 64, 64)], sems.at[orbital, part]
        )

    def place(orbital, half):
        return pltpu.make_async_copy(
            wide.at[orbital, half], out.at[orbital, pl.ds(half * 192, 64)], sems.at[orbital, half * 3]
        )

    for orbital in range(2):
        for part in (1, 2):
            clear(orbital, part).start()

    @pl.when(jnp.logical_not(is_owner))
    def _():
        for orbital in range(2):
            for part in (0, 3):
                clear(orbital, part).start()
            for part in (0, 3):
                clear(orbital, part).wait()

    @pl.when(is_owner)
    def _():
        near = lax.broadcasted_iota(jnp.int32, (64, 32, 128), 2) < 64
        for orbital in range(2):
            for half in range(2):
                block = value[orbital, half * 64 : half * 64 + 64].astype(jnp.float32)
                wide[orbital, half, :, :, :128] = jnp.where(near, block, 0.0).astype(jnp.bfloat16)
                wide[orbital, half, :, :, 128:] = jnp.where(near, 0.0, block).astype(jnp.bfloat16)
                place(orbital, half).start()
        for orbital in range(2):
            for half in range(2):
                place(orbital, half).wait()

    for orbital in range(2):
        for part in (1, 2):
            clear(orbital, part).wait()


def pad(value, shape):
    return pl.pallas_call(
        pad_kernel,
        out_shape=jax.ShapeDtypeStruct(shape, jnp.bfloat16),
        in_specs=[pl.BlockSpec(memory_space=pltpu.VMEM)],
        out_specs=pl.BlockSpec(memory_space=pl.ANY),
        scratch_shapes=[
            pltpu.VMEM((64, 32, 256), jnp.bfloat16),
            pltpu.VMEM((2, 2, 64, 32, 256), jnp.bfloat16),
            pltpu.SemaphoreType.DMA((2, 4)),
        ],
        compiler_params=pltpu.CompilerParams(vmem_limit_bytes=VMEM_BYTES),
        name="pad",
    )(value)


def line_of_chips(coeff, sphere, potential, proj_values, tile_cell, tile_atom, tile_count, dion):
    table = cas_table(256)
    table_out = jnp.concatenate([table[:64], table[192:]], axis=0)
    smem = pl.BlockSpec(memory_space=pltpu.SMEM)
    vmem = pl.BlockSpec(memory_space=pltpu.VMEM)
    anywhere = pl.BlockSpec(memory_space=pl.ANY)
    dma = pltpu.SemaphoreType.DMA
    half, single = jnp.bfloat16, jnp.float32
    result = pl.pallas_call(
        kernel,
        out_shape=jax.ShapeDtypeStruct((2, 128, 32, 128), half),
        in_specs=[smem] * 3 + [vmem] * 5 + [anywhere] * 3,
        out_specs=anywhere,
        scratch_shapes=[
            pltpu.VMEM((2, 128, 32, 256), half),
            pltpu.VMEM((128, 32, 256), jnp.int32),
            pltpu.VMEM((32, 256, 256), single),
            pltpu.VMEM((2, 256, 32, 128), half),
            pltpu.VMEM((2, 32, 128, 128), half),
            pltpu.VMEM((16384, 128), single),
            pltpu.VMEM((4, 512, 128), half),
            pltpu.VMEM((4, 512, 128), single),
            pltpu.VMEM((32, 128, 128), half),
            pltpu.VMEM((512, 128), single),
            pltpu.VMEM((512, 128), single),
            pltpu.VMEM((512, 128), single),
            pltpu.VMEM((512, 128), single),
            pltpu.VMEM((2, 8, 4, 128), single),
            pltpu.VMEM((16, 128, 128), single),
            pltpu.VMEM((2, 2, 4, 32, 16, 128), half),
            pltpu.VMEM((2, 32, 256, 128), half),
            pltpu.VMEM((2, 32, 32, 128), half),
            pltpu.VMEM((128, 32, 128), single),
            pltpu.VMEM((2, 128, 32, 128), single),
            dma((4, 2)),
            dma((2,)),
            dma((4,)),
            dma((4,)),
            dma((2, 8)),
            dma((2, 4)),
            dma((2, 8)),
            dma((2, 8)),
            dma((2, 2, 4)),
            dma((2, 2, 8)),
            dma((3, 2)),
        ],
        compiler_params=pltpu.CompilerParams(
            collective_id=0, has_side_effects=True, vmem_limit_bytes=VMEM_BYTES
        ),
        name="hamiltonian",
    )(
        tile_cell,
        tile_count,
        dion,
        tile_cell[None, :],
        tile_atom[None, :],
        proj_values.reshape(512, 128),
        table_out.T,
        table_out,
        coeff,
        sphere,
        potential,
    )
    return pad(result, coeff.shape)


def local(*values):
    coeff, slots, shards = values[0], values[4].shape[0], lax.axis_size("fft")
    if coeff.shape == (2, 256, 32, 256) and shards == 8 and slots == 512:
        return line_of_chips(*values)
    return general(*values)


def solution(mesh):
    in_specs = (
        P("band", None, "fft", None),
        P(None, "fft", None),
        P("fft", None, None),
        P("fft", None, "band"),
        P("fft"),
        P("fft"),
        P("fft"),
        P(),
    )
    out_specs = P("band", None, "fft", None)
    return jax.shard_map(local, mesh=mesh, in_specs=in_specs, out_specs=out_specs, check_vma=False)
```

```python
import math

import jax
import jax.numpy as jnp
from jax import lax
from jax.experimental import pallas as pl
from jax.experimental.pallas import tpu as pltpu
from jax.sharding import PartitionSpec as P

APD = 16
REACH = 3
MESH = pl.DeviceIdType.MESH
VMEM_BYTES = 58 * 2**20


def from_behind(value, axis, steps):
    count = lax.axis_size(axis)
    pairs = [(source, (source + steps) % count) for source in range(count)]
    return lax.ppermute(value, axis, pairs)


def cas_table(length):
    index = jnp.arange(length, dtype=jnp.int32)
    product = index[:, None] * index[None, :] % length
    angle = product.astype(jnp.float32) * (2.0 * math.pi / length)
    return ((jnp.cos(angle) + jnp.sin(angle)) * (1.0 / math.sqrt(length))).astype(jnp.bfloat16)


def frequency(index, length):
    return jnp.minimum(index, length - index)


def general(coeff, sphere, potential, proj_values, tile_cell, tile_atom, tile_count, dion):
    high = lax.Precision.HIGHEST
    orbitals, full_x, local_y, full_z = coeff.shape
    shards = lax.axis_size("fft")
    own_index = lax.axis_index("fft")
    full_y = local_y * shards
    table_x = cas_table(full_x)
    table_y = cas_table(full_y)
    table_z = cas_table(full_z)
    sphere_real = sphere.astype(jnp.float32)
    masked = (coeff.astype(jnp.float32) * sphere_real[None]).astype(jnp.bfloat16)
    row_x = frequency(jnp.arange(full_x, dtype=jnp.int32), full_x).astype(jnp.float32)
    row_y = frequency(own_index * local_y + jnp.arange(local_y, dtype=jnp.int32), full_y).astype(
        jnp.float32
    )
    row_z = frequency(jnp.arange(full_z, dtype=jnp.int32), full_z).astype(jnp.float32)
    kinetic = 2.0 * (
        (4.0 * row_x / full_x)[:, None, None] ** 2
        + (4.0 * row_y / full_y)[None, :, None] ** 2
        + (4.0 * row_z / full_z)[None, None, :] ** 2
    )
    section_one = jnp.einsum(
        "ax,oxyz->oayz", table_x, masked, preferred_element_type=jnp.float32
    ).astype(jnp.bfloat16)
    along_y = jnp.einsum(
        "by,oxyz->oxbz",
        table_y,
        lax.all_to_all(section_one, "fft", split_axis=1, concat_axis=2, tiled=True),
        preferred_element_type=jnp.float32,
    ).astype(jnp.bfloat16)
    real = jnp.dot(along_y, table_z, preferred_element_type=jnp.float32).astype(jnp.bfloat16)
    whole_proj = lax.all_gather(proj_values, "band", axis=2, tiled=True)
    flat = real.reshape(orbitals, -1, 128)
    patches = jnp.take(flat, tile_cell, axis=1)
    slots = tile_cell.shape[0]
    live = (jnp.arange(slots, dtype=jnp.int32) < tile_count[0]).astype(jnp.float32)
    partial_value = (
        jnp.einsum("otc,tpc->otp", patches, whole_proj, preferred_element_type=jnp.float32)
        * live[None, :, None]
    )
    width = (2 * REACH + 1) * APD
    home = tile_atom // APD
    local_atom = (home - own_index + REACH) % shards * APD + tile_atom % APD
    onehot = (local_atom[:, None] == jnp.arange(width, dtype=jnp.int32)[None, :]).astype(
        jnp.float32
    )
    table = jnp.einsum("otp,ta->oap", partial_value, onehot, precision=high)
    intersection = table
    for offset in range(-2 * REACH, 2 * REACH + 1):
        if offset != 0:
            arrived = from_behind(table, "fft", offset)
            first = max(0, -offset)
            last = min(2 * REACH, 2 * REACH - offset)
            intersection = intersection.at[:, first * APD : (last + 1) * APD].add(
                arrived[:, (first + offset) * APD : (last + offset + 1) * APD]
            )
    weights = intersection * dion[None, None, :]
    back = jnp.einsum("oap,ta->otp", weights, onehot, precision=high) * live[None, :, None]
    added = jnp.einsum("otp,tpc->otc", back, whole_proj.astype(jnp.float32), precision=high)
    nonlocal_part = (
        jnp.zeros(flat.shape, jnp.float32).at[:, tile_cell].add(added).reshape(real.shape)
    )
    mixed = (potential[None] * real.astype(jnp.float32) + nonlocal_part).astype(jnp.bfloat16)
    section_three = jnp.dot(mixed, table_z, preferred_element_type=jnp.float32).astype(jnp.bfloat16)
    section_four = jnp.einsum(
        "by,oxyz->oxbz", table_y, section_three, preferred_element_type=jnp.float32
    ).astype(jnp.bfloat16)
    spectrum = jnp.einsum(
        "ax,oxyz->oayz",
        table_x,
        lax.all_to_all(section_four, "fft", split_axis=2, concat_axis=1, tiled=True),
        preferred_element_type=jnp.float32,
    )
    result = sphere_real[None] * (spectrum + kinetic[None] * masked.astype(jnp.float32))
    return result.astype(jnp.bfloat16)


def remote(source, target, send_sem, recv_sem, device, axis="fft"):
    return pltpu.make_async_remote_copy(
        src_ref=source,
        dst_ref=target,
        send_sem=send_sem,
        recv_sem=recv_sem,
        device_id={axis: device},
        device_id_type=MESH,
    )


def greet(device, axis="fft"):
    pl.semaphore_signal(
        pltpu.get_barrier_semaphore(), inc=1, device_id={axis: device}, device_id_type=MESH
    )


OWNERS = (0, 1, 6, 7)
EARLY = 4
HIGH = lax.Precision.HIGHEST


def matmul(left, right):
    return jnp.dot(left, right, preferred_element_type=jnp.float32)


def exact(left, right, dims=((1,), (0,))):
    return lax.dot_general(
        left, right, (dims, ((), ())), precision=HIGH, preferred_element_type=jnp.float32
    )


def swap(value):
    return jnp.transpose(value, (1, 0, 2))


def slab(at):
    return pl.ds(pl.multiple_of(at * 32, 32), 32)


def kernel(
    cell, count, dion, cell_row, atom_row, own_proj, table_in, table_out, coeff, sphere, potential,
    out,
    waves, ball, field, first, rows, cells, proj_parts, proj, spots, patches, tiles,
    planes_of, slot_atom, tables, fourth, back, gathered, ready, inside, kinetic,
    load_sem, out_sem, proj_send, proj_recv, first_send, first_recv, table_send, table_recv,
    back_send, back_recv, keep_sem,
):
    me, band = lax.axis_index("fft"), lax.axis_index("band")
    is_owner = (me < 2) | (me >= 6)
    own_block = jnp.where(me < 2, me, me - 4)

    def load_waves(orbital, half):
        return pltpu.make_async_copy(
            coeff.at[orbital, pl.ds(half * 192, 64)],
            waves.at[orbital, pl.ds(half * 64, 64)],
            load_sem.at[orbital, half],
        )

    def load_ball(half):
        return pltpu.make_async_copy(
            sphere.at[pl.ds(half * 192, 64)], ball.at[pl.ds(half * 64, 64)], load_sem.at[2, half]
        )

    load_field = pltpu.make_async_copy(potential, field, load_sem.at[3, 0])

    @pl.when(is_owner)
    def _():
        for half in range(2):
            load_ball(half).start()
            load_waves(0, half).start()
        for half in range(2):
            load_waves(1, half).start()

    for step in range(1, 8):
        greet((me + step) % 8)
    for step in range(1, 4):
        greet((band + step) % 4, "band")
    pl.semaphore_wait(pltpu.get_barrier_semaphore(), 10)

    def send_proj(step):
        return remote(
            own_proj,
            proj_parts.at[band],
            proj_send.at[step],
            proj_recv.at[step],
            (band + step) % 4,
            "band",
        )

    for step in range(1, 4):
        send_proj(step).start()

    def slot(orbital, at):
        return rows.at[orbital, :, slab(at)]

    def send_first(orbital, step):
        there = (me + step) % 8
        return remote(
            first.at[orbital, slab(there)],
            slot(orbital, own_block),
            first_send.at[orbital, step],
            first_recv.at[orbital, own_block],
            there,
        )

    def keep_first(orbital):
        return pltpu.make_async_copy(
            first.at[orbital, slab(me)], slot(orbital, own_block), keep_sem.at[0, orbital]
        )

    def section(orbital, carry):
        near = lax.broadcasted_iota(jnp.int32, (64, 32, 128), 2) < 64
        for half in range(2):
            load_waves(orbital, half).wait()
            part = pl.ds(half * 64, 64)
            value = waves[orbital, part].astype(jnp.float32) * ball[part].astype(jnp.float32)
            value = jnp.where(near, value[..., :128], value[..., 128:])
            spots[:, part, :] = swap(value).astype(jnp.bfloat16)

        def along_x(block, inner):
            part = pl.ds(pl.multiple_of(block * 64, 64), 64)
            table = table_in[part, :]
            for group in range(2):
                found = [matmul(table, spots[group * 16 + k]) for k in range(16)]
                value = swap(jnp.stack(found)).astype(jnp.bfloat16)
                first[orbital, part, group * 16 : group * 16 + 16, :] = value
            return inner

        lax.fori_loop(0, 4, along_x, 0)
        keep_first(orbital).start()

        @pl.when(orbital == 0)
        def _():
            for step in range(1, 8):
                send_first(orbital, step).start()

        return carry

    @pl.when(is_owner)
    def _():
        for half in range(2):
            load_ball(half).wait()
        lax.fori_loop(0, 2, section, 0)

    load_field.start()

    cells_at = cell_row[...]
    in_plane = (cells_at & 1) * 256 + ((cells_at & 511) >> 1)
    at_row = lax.broadcasted_iota(jnp.int32, (512, 512), 0)
    patches_at = (at_row == in_plane).astype(jnp.float32)
    tables_row = patches_at.astype(jnp.bfloat16)
    planes_row = jnp.broadcast_to((cells_at >> 9).astype(jnp.float32), (128, 512))
    planes_of[...] = jnp.transpose(planes_row, (1, 0))
    atoms = lax.broadcasted_iota(jnp.int32, (128, 512), 0)
    slots = lax.broadcasted_iota(jnp.int32, (128, 512), 1)
    chosen = ((atoms == atom_row[...]) & (slots < count[0])).astype(jnp.float32)
    slot_atom[...] = jnp.transpose(chosen, (1, 0))
    proj_parts[band] = own_proj[...]
    for step in range(1, 4):
        source = proj_parts.at[(band + 4 - step) % 4]
        copy = remote(
            own_proj, source, proj_send.at[step], proj_recv.at[step], (band + step) % 4, "band"
        )
        copy.wait_recv()
        copy.wait_send()
    lane_in = lax.broadcasted_iota(jnp.int32, (128, 128), 0)
    lane_out = lax.broadcasted_iota(jnp.int32, (128, 128), 1)
    for p in range(4):
        whole = jnp.zeros((512, 128), jnp.float32)
        for part in range(4):
            wanted = (lane_in == lane_out + 32 * (p - part)) & (lane_out // 32 == part)
            move = wanted.astype(jnp.float32).astype(jnp.bfloat16)
            whole = whole + matmul(proj_parts[part], move)
        proj[p] = whole
    load_field.wait()

    def squares(start, shape, axis):
        at = lax.broadcasted_iota(jnp.int32, shape, axis) + start
        return (frequency(at, 256).astype(jnp.float32) * (4.0 / 256)) ** 2

    def inner(value):
        near = lax.broadcasted_iota(jnp.int32, value.shape[:-1] + (128,), 2) < 64
        return jnp.where(near, value[..., :128], value[..., 128:])

    def kinetic_term(block, carry):
        lane = lax.broadcasted_iota(jnp.int32, (1, 1, 128), 2)
        lane_freq = jnp.where(lane < 64, lane, 128 - lane).astype(jnp.float32) * (4.0 / 256)
        energy = 2.0 * (
            squares(block * 32 + block // 2 * 128, (32, 1, 128), 0)
            + squares(me * 32, (1, 32, 128), 1)
            + lane_freq**2
        )
        near_ball = inner(ball[slab(block)].astype(jnp.float32))
        inside[slab(block)] = near_ball
        for orbital in range(2):
            masked = inner(waves[orbital, slab(block)].astype(jnp.float32)) * near_ball
            kinetic[orbital, slab(block)] = energy * masked
        return carry

    @pl.when(is_owner)
    def _():
        lax.fori_loop(0, 4, kinetic_term, 0)
        for step in range(1, 8):
            send_first(0, step).wait_send()
        for step in range(1, EARLY):
            send_first(1, step).start()

    def send_table(orbital, step):
        return remote(
            tables.at[orbital, me],
            tables.at[orbital, me],
            table_send.at[orbital, step],
            table_recv.at[orbital, step],
            (me + step) % 8,
        )

    def slots_back(orbital, device, part):
        return gathered.at[orbital, :, pl.ds(pl.multiple_of(device * 32 + part * 16, 16), 16)]

    def send_back(orbital, part, block, owner):
        return remote(
            back.at[orbital, part, block],
            slots_back(orbital, me, part),
            back_send.at[orbital, part, block],
            back_recv.at[orbital, part, me],
            owner,
        )

    def keep_back(orbital, part, block):
        return pltpu.make_async_copy(
            back.at[orbital, part, block],
            slots_back(orbital, me, part),
            keep_sem.at[1 + part, orbital],
        )

    def one_orbital(orbital, carry):
        for at, owner in enumerate(OWNERS):

            @pl.when(me != owner)
            def _(at=at, owner=owner):
                remote(
                    first.at[orbital, slab(0)],
                    slot(orbital, at),
                    first_send.at[orbital, 0],
                    first_recv.at[orbital, at],
                    owner,
                ).wait_recv()

        @pl.when(is_owner)
        def _():
            keep_first(orbital).wait()

        def to_plane(x, inner):
            second = matmul(table_in[...], rows[orbital, x]).astype(jnp.bfloat16)
            wide = matmul(second, table_out[...]).astype(jnp.bfloat16).astype(jnp.float32)
            base = pl.multiple_of(x * 512, 512)
            cells[pl.ds(base, 256), :] = wide[:, :128]
            cells[pl.ds(base + 256, 256), :] = wide[:, 128:]
            return inner

        lax.fori_loop(0, 32, to_plane, 0, unroll=4)

        def fetch(group, inner):
            base = pl.multiple_of(group * 8, 8)
            for k in range(8):
                at = cell[base + k]
                row = (at >> 9) * 512 + (at & 1) * 256 + ((at & 511) >> 1)
                patches[pl.ds(base + k, 1), :] = cells[pl.ds(row, 1), :]
            return inner

        lax.fori_loop(0, 64, fetch, 0)
        of_slot = slot_atom[...]
        ones = jnp.ones((8, 128), jnp.float32)
        for p in range(4):
            by_atom = exact(chosen, patches[...] * proj[p])
            tables[orbital, me, p : p + 1, :] = exact(ones, by_atom, ((1,), (1,)))[0:1]
        for step in range(1, 8):
            send_table(orbital, step).start()

        @pl.when(is_owner & (orbital == 0))
        def _():
            for step in range(EARLY, 8):
                send_first(1, step).start()

        for step in range(1, 8):
            source = tables.at[orbital, (me + 8 - step) % 8]
            copy = remote(
                source,
                source,
                table_send.at[orbital, step],
                table_recv.at[orbital, step],
                (me + step) % 8,
            )
            copy.wait_recv()
            copy.wait_send()
        total = tables[orbital, 0]
        for other in range(1, 8):
            total = total + tables[orbital, other]
        strength = exact(of_slot, jnp.concatenate([total, total], axis=0), ((1,), (1,)))
        added = strength[:, 0:1] * dion[0] * proj[0]
        for p in range(1, 4):
            added = added + strength[:, p : p + 1] * dion[p] * proj[p]
        tiles[...] = added

        def from_planes(pair, inner):
            pieces = [
                jnp.where(planes_of[...] == (2 * pair + k).astype(jnp.float32), tiles[...], 0.0)
                for k in range(2)
            ]
            pieces = jnp.concatenate([piece.astype(jnp.bfloat16) for piece in pieces], axis=1)
            both = matmul(tables_row, pieces)
            for k in range(2):
                from_plane(2 * pair + k, both[:, k * 128 : k * 128 + 128])
            return inner

        def from_plane(x, spread):
            base = pl.multiple_of(x * 512, 512)
            level = field[x]
            left = level[:, :128] * cells[pl.ds(base, 256), :] + spread[:256]
            right = level[:, 128:] * cells[pl.ds(base + 256, 256), :] + spread[256:]
            mixed = jnp.concatenate([left.astype(jnp.bfloat16), right.astype(jnp.bfloat16)], axis=1)
            third = matmul(mixed, table_in[...]).astype(jnp.bfloat16)
            fourth[x % 16] = matmul(table_out[...], third)

        def half_slab(part, inner):
            lax.fori_loop(0, 8, lambda x, c: from_planes(part * 8 + x, c), 0, unroll=2)

            def turn(group, inmost):
                value = fourth[:, pl.ds(pl.multiple_of(group * 8, 8), 8), :]
                value = swap(value).astype(jnp.bfloat16)
                back[orbital, part, group // 4, pl.ds(group % 4 * 8, 8)] = value
                return inmost

            lax.fori_loop(0, 16, turn, 0, unroll=2)
            for block, owner in enumerate(OWNERS):

                @pl.when(me != owner)
                def _(block=block, owner=owner):
                    send_back(orbital, part, block, owner).start()

                @pl.when(me == owner)
                def _(block=block):
                    keep_back(orbital, part, block).start()

            return inner

        lax.fori_loop(0, 2, half_slab, 0)
        return carry

    lax.fori_loop(0, 2, one_orbital, 0)

    def write(step):
        return pltpu.make_async_copy(
            ready.at[step % 2], out.at[step // 4, slab(step % 4)], out_sem.at[step % 2]
        )

    def finish(step, carry):
        orbital, block = step // 4, step % 4

        @pl.when(block == 0)
        def _():
            for part in range(2):
                for other in range(1, 8):
                    sender = (me + other) % 8
                    remote(
                        back.at[orbital, part, 0],
                        slots_back(orbital, sender, part),
                        back_send.at[orbital, part, 0],
                        back_recv.at[orbital, part, sender],
                        sender,
                    ).wait_recv()
                keep_back(orbital, part, own_block).wait()

        @pl.when(step >= 2)
        def _():
            write(step - 2).wait()

        table = table_out[slab(block), :]
        for group in range(2):
            here = slice(group * 16, group * 16 + 16)
            found = [matmul(table, gathered[orbital, group * 16 + k]) for k in range(16)]
            spectrum = swap(jnp.stack(found))
            result = inside[slab(block), here] * spectrum + kinetic[orbital, slab(block), here]
            ready[step % 2, :, here] = result.astype(jnp.bfloat16)
        write(step).start()
        return carry

    @pl.when(is_owner)
    def _():
        lax.fori_loop(0, 8, finish, 0)
        write(6).wait()
        write(7).wait()
        for step in range(1, 8):
            send_first(1, step).wait_send()

    for orbital in range(2):
        for part in range(2):
            for block, owner in enumerate(OWNERS):

                @pl.when(me != owner)
                def _(orbital=orbital, part=part, block=block, owner=owner):
                    send_back(orbital, part, block, owner).wait_send()


def pad_kernel(value, out, empty, wide, sems):
    me = lax.axis_index("fft")
    is_owner = (me < 2) | (me >= 6)
    empty[...] = jnp.zeros_like(empty)

    def clear(orbital, part):
        return pltpu.make_async_copy(
            empty, out.at[orbital, pl.ds(part * 64, 64)], sems.at[orbital, part]
        )

    def place(orbital, half):
        return pltpu.make_async_copy(
            wide.at[orbital, half], out.at[orbital, pl.ds(half * 192, 64)], sems.at[orbital, half * 3]
        )

    for orbital in range(2):
        for part in (1, 2):
            clear(orbital, part).start()

    @pl.when(jnp.logical_not(is_owner))
    def _():
        for orbital in range(2):
            for part in (0, 3):
                clear(orbital, part).start()
            for part in (0, 3):
                clear(orbital, part).wait()

    @pl.when(is_owner)
    def _():
        near = lax.broadcasted_iota(jnp.int32, (64, 32, 128), 2) < 64
        for orbital in range(2):
            for half in range(2):
                block = value[orbital, half * 64 : half * 64 + 64].astype(jnp.float32)
                wide[orbital, half, :, :, :128] = jnp.where(near, block, 0.0).astype(jnp.bfloat16)
                wide[orbital, half, :, :, 128:] = jnp.where(near, 0.0, block).astype(jnp.bfloat16)
                place(orbital, half).start()
        for orbital in range(2):
            for half in range(2):
                place(orbital, half).wait()

    for orbital in range(2):
        for part in (1, 2):
            clear(orbital, part).wait()


def pad(value, shape):
    return pl.pallas_call(
        pad_kernel,
        out_shape=jax.ShapeDtypeStruct(shape, jnp.bfloat16),
        in_specs=[pl.BlockSpec(memory_space=pltpu.VMEM)],
        out_specs=pl.BlockSpec(memory_space=pl.ANY),
        scratch_shapes=[
            pltpu.VMEM((64, 32, 256), jnp.bfloat16),
            pltpu.VMEM((2, 2, 64, 32, 256), jnp.bfloat16),
            pltpu.SemaphoreType.DMA((2, 4)),
        ],
        compiler_params=pltpu.CompilerParams(vmem_limit_bytes=VMEM_BYTES),
        name="pad",
    )(value)


def line_of_chips(coeff, sphere, potential, proj_values, tile_cell, tile_atom, tile_count, dion):
    table = cas_table(256)
    table_out = jnp.concatenate([table[:64], table[192:]], axis=0)
    smem = pl.BlockSpec(memory_space=pltpu.SMEM)
    vmem = pl.BlockSpec(memory_space=pltpu.VMEM)
    anywhere = pl.BlockSpec(memory_space=pl.ANY)
    dma = pltpu.SemaphoreType.DMA
    half, single = jnp.bfloat16, jnp.float32
    result = pl.pallas_call(
        kernel,
        out_shape=jax.ShapeDtypeStruct((2, 128, 32, 128), half),
        in_specs=[smem] * 3 + [vmem] * 5 + [anywhere] * 3,
        out_specs=anywhere,
        scratch_shapes=[
            pltpu.VMEM((2, 128, 32, 256), half),
            pltpu.VMEM((128, 32, 256), jnp.int32),
            pltpu.VMEM((32, 256, 256), single),
            pltpu.VMEM((2, 256, 32, 128), half),
            pltpu.VMEM((2, 32, 128, 128), half),
            pltpu.VMEM((16384, 128), single),
            pltpu.VMEM((4, 512, 128), half),
            pltpu.VMEM((4, 512, 128), single),
            pltpu.VMEM((32, 128, 128), half),
            pltpu.VMEM((512, 128), single),
            pltpu.VMEM((512, 128), single),
            pltpu.VMEM((512, 128), single),
            pltpu.VMEM((512, 128), single),
            pltpu.VMEM((2, 8, 4, 128), single),
            pltpu.VMEM((16, 128, 128), single),
            pltpu.VMEM((2, 2, 4, 32, 16, 128), half),
            pltpu.VMEM((2, 32, 256, 128), half),
            pltpu.VMEM((2, 32, 32, 128), half),
            pltpu.VMEM((128, 32, 128), single),
            pltpu.VMEM((2, 128, 32, 128), single),
            dma((4, 2)),
            dma((2,)),
            dma((4,)),
            dma((4,)),
            dma((2, 8)),
            dma((2, 4)),
            dma((2, 8)),
            dma((2, 8)),
            dma((2, 2, 4)),
            dma((2, 2, 8)),
            dma((3, 2)),
        ],
        compiler_params=pltpu.CompilerParams(
            collective_id=0, has_side_effects=True, vmem_limit_bytes=VMEM_BYTES
        ),
        name="hamiltonian",
    )(
        tile_cell,
        tile_count,
        dion,
        tile_cell[None, :],
        tile_atom[None, :],
        proj_values.reshape(512, 128),
        table_out.T,
        table_out,
        coeff,
        sphere,
        potential,
    )
    return pad(result, coeff.shape)


def local(*values):
    coeff, slots, shards = values[0], values[4].shape[0], lax.axis_size("fft")
    if coeff.shape == (2, 256, 32, 256) and shards == 8 and slots == 512:
        return line_of_chips(*values)
    return general(*values)


def solution(mesh):
    in_specs = (
        P("band", None, "fft", None),
        P(None, "fft", None),
        P("fft", None, None),
        P("fft", None, "band"),
        P("fft"),
        P("fft"),
        P("fft"),
        P(),
    )
    out_specs = P("band", None, "fft", None)
    return jax.shard_map(local, mesh=mesh, in_specs=in_specs, out_specs=out_specs, check_vma=False)
```
